128 devices in a mesh: lat: 8 (over y, z_hi), lon: 16 (over x, z_lo, core).
Axes of the slice: x: 4, y: 4, z: 4 (z_hi: 2, z_lo: 2; z = z_hi * 2 + z_lo), core: 2. Of those that a mesh axis runs over, the one named last changes fastest.
Arguments:
- humidity: bfloat16 [137, 1024, 2048], P(None, 'lat', 'lon'), may hold values from 0.099609375 to 10
- wind_u: bfloat16 [137, 1024, 2048], P(None, 'lat', 'lon'), may hold values from -6 to 6
- wind_v: bfloat16 [137, 1024, 2048], P(None, 'lat', 'lon'), may hold values from -6 to 6
- weights: float32 [137], replicated, may hold values from 0.002 to 0.02
- labels: int32 [1024, 2048], P('lat', 'lon'), may hold values from 0 to 127, as said below
- global_labels: int32 [8, 16, 128], P('lat', 'lon'), may hold values from 0 to 4095, as said below
Outputs:
- anomaly: float32 [1024, 2048], P('lat', 'lon')
The draws below stay inside these ranges and needn't reach their ends.
Inputs may be any that keep to these rules, and one draw needn't show every extreme that they name: Each tile's labels are constant on aligned patches of 4 rows by 8 columns. `global_labels`: each of the 4096 global objects is named by exactly 4 entries. The tiles form groups of four: tile row i or i plus half of 8, with tile column j or j plus 1 for even j. All entries that name one object lie in one such group.
All inputs are finite; a program needn't handle non-finite values.
Results may differ from the reference program's by a relative error of at most 0.0039.
Values may be sent and summed in bfloat16 or wider, within the bound.
No kernel may reach another device: no remote copies, remote signals or barrier semaphores. Data moves between devices by JAX's collectives and lax.ppermute only.
A program may use at most 128 MiB of HBM per device.

```python
import math
import jax
import jax.numpy as jnp
from jax import lax

LEVELS = 137
LAT_DEV = 128
LON_DEV = 128
LOCAL = 128
TLAT = 8
TLON = 16
LAT = 1024
LON = 2048
OBJECTS = 4096


def draw_labels(key, part):
    key = jax.random.fold_in(key, 11)
    coarse = jax.random.randint(key, (LAT // 4, LON // 8), 0, LOCAL)
    return jnp.repeat(jnp.repeat(coarse, 4, axis=0), 8, axis=1).astype(jnp.int32)


def draw_global_labels(key, part):
    key = jax.random.fold_in(key, 23)
    half_rows = TLAT // 2
    half_cols = TLON // 2
    block_count = half_rows * half_cols
    block_keys = jax.random.split(key, block_count)
    shuffled = jax.vmap(lambda k: jax.random.permutation(k, 4 * LOCAL))(block_keys)
    block_ids = jnp.arange(block_count, dtype=jnp.int32)
    members = (shuffled % LOCAL + block_ids[:, None] * LOCAL).astype(jnp.int32)
    members = members.reshape(block_count, 4, LOCAL)
    tile_rows = jnp.arange(TLAT, dtype=jnp.int32)
    tile_cols = jnp.arange(TLON, dtype=jnp.int32)
    block_of = tile_rows[:, None] % half_rows * half_cols + tile_cols[None, :] // 2
    slot_of = tile_rows[:, None] // half_rows * 2 + tile_cols[None, :] % 2
    return members[block_of, slot_of].astype(jnp.int32)


def steps_of(own_key, shape, pieces, smallest, high):
    level = 1.0
    for position, shards_of in pieces:
        draws = jax.random.uniform(jax.random.fold_in(jax.random.fold_in(own_key, 6), position), (shards_of,), jnp.float32, smallest / len(pieces), high / len(pieces))
        level = level * jnp.repeat(jnp.exp(draws), shape[position] // shards_of).reshape((-1,) + (1,) * (len(shape) - 1 - position))
    return level


def gaussian(rng, dims, width, bound, shards=(), kind=jnp.bfloat16):
    drawn = width * jax.random.normal(rng, dims, jnp.float32)
    if shards:
        drawn = drawn * steps_of(rng, dims, shards, -0.22, 0.18)
    return jnp.clip(drawn, -bound, bound).astype(kind)


def setup_inputs(seed: int = 0) -> dict:
    streams_of = jax.random.split(jax.random.key(seed), 7)
    return {
        "humidity": jnp.clip(jnp.exp(math.log(10.0) - 4.609084 * jax.random.uniform(streams_of[0], (LEVELS, LAT, LON), jnp.float32) ** steps_of(streams_of[0], (LEVELS, LAT, LON), ((1, 8), (2, 16)), -0.2, 0.2)), 0.099609375, 10.0).astype(jnp.bfloat16),
        "wind_u": gaussian(streams_of[1], (LEVELS, LAT, LON), 1.0, 6.0, ((1, 8), (2, 16))),
        "wind_v": gaussian(streams_of[2], (LEVELS, LAT, LON), 1.0, 6.0, ((1, 8), (2, 16))),
        "weights": jnp.clip(jnp.exp(jax.random.uniform(streams_of[3], (LEVELS,), jnp.float32, math.log(0.002), math.log(0.02))), 0.002, 0.02),
        "labels": draw_labels(jax.random.fold_in(streams_of[6], 71), 0),
        "global_labels": draw_global_labels(jax.random.fold_in(streams_of[6], 71), 0),
    }


def reference(humidity, wind_u, wind_v, weights, labels, global_labels):
    wind_speed = jnp.sqrt(wind_u.astype(jnp.float32) ** 2 + wind_v.astype(jnp.float32) ** 2 + 1.0)
    transport = humidity.astype(jnp.float32) * wind_speed
    transport = lax.optimization_barrier(transport.astype(jnp.bfloat16)).astype(jnp.float32)
    padded = jnp.pad(transport, ((0, 0), (1, 1), (0, 0)))
    smooth = 0.5 * transport + 0.125 * (padded[:, :-2, :] + padded[:, 2:, :] + jnp.roll(transport, 1, axis=2) + jnp.roll(transport, -1, axis=2))
    smoothed = lax.optimization_barrier(smooth.astype(jnp.bfloat16)).astype(jnp.float32)
    row_tile = (jnp.arange(LAT) // LAT_DEV).astype(jnp.int32)
    col_tile = (jnp.arange(LON) // LON_DEV).astype(jnp.int32)
    objects = global_labels[row_tile[:, None], col_tile[None, :], labels].reshape(-1)
    columns_flat = smoothed.reshape(LEVELS, -1)
    totals = jax.ops.segment_sum(columns_flat.T, objects, num_segments=OBJECTS)
    counts = jax.ops.segment_sum(jnp.ones(objects.shape, jnp.float32), objects, num_segments=OBJECTS)
    profile = totals / jnp.maximum(counts, 1.0)[:, None]
    energy = lax.optimization_barrier(jnp.sum(weights[None, :] * profile * profile, axis=1))
    departure = columns_flat - profile[objects].T
    spread = lax.optimization_barrier(jnp.sum(weights[:, None] * departure * departure, axis=0))
    return jnp.sqrt(spread / energy[objects]).reshape(LAT, LON)
```

```python
import jax
import jax.numpy as jnp
from jax import lax
from jax.experimental import pallas as pl
from jax.experimental.pallas import tpu as pltpu
from jax.sharding import PartitionSpec as P

F32 = jnp.float32
BF16 = jnp.bfloat16
LEV = 137
KP = 152
N = 128
CHUNKS = ((0, 8), (8, 16), (24, 24), (48, 24), (72, 24), (96, 24), (120, 8), (128, 9))
NT = (((1,), (1,)), ((), ()))
NN = (((1,), (0,)), ((), ()))


def iota(shape, dim):
    return lax.broadcasted_iota(jnp.int32, shape, dim)


def dot(a, b, dims):
    return lax.dot_general(a, b, dims, preferred_element_type=F32)


def column(row, rows):
    shape = (rows, row.shape[1])
    return jnp.sum(jnp.where(iota(shape, 0) == iota(shape, 1), row, 0.0), axis=1, keepdims=True)


def ends():
    shape = (16, N)
    first = (iota(shape, 0) == 0) & (iota(shape, 1) == 0)
    last = (iota(shape, 0) == 1) & (iota(shape, 1) == N - 1)
    return jnp.where(first | last, 1.0, 0.0).astype(BF16)


def halos(r0, r1, rc, ro):
    i, j = lax.axis_index("lat"), lax.axis_index("lon")
    i_even, j_even = lax.rem(i, 2) == 0, lax.rem(j, 2) == 0
    r0, r1, rc, ro = (r[...].astype(F32) for r in (r0, r1, rc, ro))
    north = jnp.where(i == 0, 0.0, jnp.where(i_even, r1, r0))
    south = jnp.where(i == 7, 0.0, jnp.where(i_even, r0, r1))
    west = jnp.where(j_even, ro, rc)
    east = jnp.where(j_even, rc, ro)
    return north, south, west, east


def transport_kernel(h_hbm, u_hbm, v_hbm, t_ref, s0_ref, s1_ref, c0_ref, c1_ref, hb, ub, vb, cols, sems):
    copies = []
    for c, (a, n) in enumerate(CHUNKS):
        row = []
        for m, (src, dst) in enumerate(((h_hbm, hb), (u_hbm, ub), (v_hbm, vb))):
            copy = pltpu.make_async_copy(src.at[pl.ds(a, n)], dst.at[pl.ds(a, n)], sems.at[c, m])
            copy.start()
            row.append(copy)
        copies.append(row)
    zeros = jnp.zeros((N, N), F32)
    for k in range(LEV, KP):
        t_ref[pl.ds(KP + k, N, stride=KP), :] = zeros
    blank = jnp.zeros((KP, N), F32)
    t_ref[pl.ds(0, KP), :] = blank
    t_ref[pl.ds((N + 1) * KP, KP), :] = blank
    cols[...] = jnp.zeros((3, N, N), BF16)
    lane = iota((N, N), 1)

    def level(k):
        parts = []
        for b in range(0, N, 32):
            rows = pl.ds(b, 32)
            u = ub[k, rows, :].astype(F32)
            v = vb[k, rows, :].astype(F32)
            x = u * u + v * v + 1.0
            t = (hb[k, rows, :].astype(F32) * (x * lax.rsqrt(x))).astype(BF16)
            t_ref[pl.ds((1 + b) * KP + k, 32, stride=KP), :] = t.astype(F32)
            parts.append(t)
        return jnp.concatenate(parts, axis=0)

    def group(k, size):
        ends = level(k)
        for q in range(1, size):
            moved = pltpu.roll(level(k + q), 2 * q, 1)
            ends = jnp.where((lane == 2 * q) | (lane == 2 * q - 1), moved, ends)
        shift = 2 * lax.rem(k, 64)
        mine = lax.rem(lane - shift + N + 1, N) < 2 * size
        block = lax.div(k, 64)
        cols[block] = jnp.where(mine, pltpu.roll(ends, shift, 1), cols[block])

    for (a, n), row in zip(CHUNKS, copies):
        for copy in row:
            copy.wait()

        def groups(g, _, a=a):
            group(a + 8 * g, 8)
            return 0

        lax.fori_loop(0, n // 8, groups, 0)
        if n % 8:
            group(a + n - n % 8, n % 8)
    i_even = lax.rem(lax.axis_index("lat"), 2) == 0
    j_even = lax.rem(lax.axis_index("lon"), 2) == 0

    def row_at(top):
        start = pl.multiple_of(jnp.where(top, KP, N * KP), 8)
        return t_ref[pl.ds(start, KP), :].astype(BF16)

    k, at = iota((KP, 3 * N), 0), iota((KP, 3 * N), 1)
    left_at = 2 * k
    right_at = jnp.where(lax.rem(k, 64) == 0, 2 * k + N - 1, 2 * k - 1)
    packed = jnp.concatenate([cols[0], cols[1], cols[2]], axis=1)

    def col_at(left):
        pick = jnp.where(at == jnp.where(left, left_at, right_at), 1.0, 0.0).astype(BF16)
        return dot(pick, packed, NT).astype(BF16)

    s0_ref[...] = row_at(jnp.logical_not(i_even))
    s1_ref[...] = row_at(i_even)
    c0_ref[...] = col_at(jnp.logical_not(j_even))
    c1_ref[...] = col_at(j_even)


def sums_kernel(t_ref, lab_ref, t0_ref, west_ref, east_ref):
    lab = lab_ref[...]
    lane = iota((N, N), 1)
    west_ref[...] = jnp.where(lane == 0, -1, pltpu.roll(lab, 1, 1))
    east_ref[...] = jnp.where(lane == N - 1, -1, pltpu.roll(lab, N - 1, 1))
    ids = iota((N, N), 0)
    t0_ref[...] = jnp.zeros((KP, N), F32)

    def patch_row(q):
        base = pl.multiple_of((1 + 4 * q) * KP, 8)
        x = [t_ref[pl.ds(base + m * KP, KP), :] for m in range(-1, 5)]
        whole = x[1] + x[2] + x[3] + x[4]
        step = jnp.where(iota((KP, N), 0) == LEV, 32.0, (x[0] - x[4]) + (x[5] - x[1]))
        left = jnp.concatenate([whole.astype(BF16), step.astype(BF16)], axis=1)
        r = pl.ds(4 * q, 1)
        here = jnp.where(lab_ref[r, :] == ids, 0.125, 0.0)
        west = jnp.where(west_ref[r, :] == ids, 0.125, 0.0)
        east = jnp.where(east_ref[r, :] == ids, 0.125, 0.0)
        spread = 6.0 * here + (west + east)
        return left, jnp.concatenate([spread.astype(BF16), here.astype(BF16)], axis=1)

    def patch_rows(i, _):
        pairs = [patch_row(16 * i + m) for m in range(16)]
        left, right = (jnp.concatenate(p, axis=1) for p in zip(*pairs))
        t0_ref[...] += dot(left, right, NT)
        return 0

    lax.fori_loop(0, N // 64, patch_rows, 0)


def pack_kernel(t0_ref, r0, r1, rc, ro, lab_ref, gl_ref, pay_ref):
    north, south, west, east = halos(r0, r1, rc, ro)
    lab = lab_ref[...].astype(F32)
    ids = iota((N, N), 0).astype(F32)
    sides = dot(ends(), lab.astype(BF16), NT)

    def marks(row):
        return jnp.where(row == ids, 0.125, 0.0)

    left = jnp.concatenate([north, south, west, east], axis=1).astype(BF16)
    right = jnp.concatenate(
        [marks(lab[0:1]), marks(lab[N - 1 : N]), marks(sides[0:1]), marks(sides[1:2])], axis=1
    ).astype(BF16)
    total = t0_ref[...] + dot(left, right, NT)
    count = total[LEV : LEV + 1] * (1.0 / 32.0)
    count_hi = jnp.floor(count * 0.125)
    gl = gl_ref[...].astype(F32)
    gl_hi = jnp.floor(gl * (1.0 / 64.0))
    row = iota((KP, N), 0)
    for m, extra in enumerate((count_hi, count - 8.0 * count_hi, gl_hi, gl - 64.0 * gl_hi)):
        total = jnp.where(row == LEV + m, extra, total)
    pay_ref[...] = total.astype(BF16)


def smooth_kernel(t_ref, r0, r1, rc, ro, w_ref, s_ref, root_ref):
    north, south, west, east = halos(r0, r1, rc, ro)
    low = iota((KP, N), 1) < 64
    sides = (
        jnp.where(low, west, pltpu.roll(east, 64, 1)).astype(BF16),
        jnp.where(low, pltpu.roll(west, 64, 1), east).astype(BF16),
    )
    root_ref[...] = jnp.sqrt(column(w_ref[...], KP)) + jnp.zeros((KP, N), F32)
    a, c = iota((2 * N, N), 0), iota((2 * N, N), 1)
    band = jnp.where(a == c, 0.5, jnp.where(jnp.abs(a - c) == 1, 0.125, 0.0))
    side = jnp.where(c == jnp.where(a < N + 64, 0, N - 1), 0.125, 0.0)
    right = jnp.where(a < N, band, side).astype(BF16)
    lane = lax.rem(iota((1, N), 1), 64)

    def at(r):
        return pl.ds(pl.multiple_of(r * KP, 8), KP)

    for half in range(2):

        def rows(i, _, half=half):
            top = 64 * half + 32 * i
            lefts = []
            for m in range(32):
                mine = jnp.where(lane == 32 * i + m, 1.0, 0.0).astype(BF16)
                lefts.append(jnp.concatenate([t_ref[at(top + m + 1), :].astype(BF16), sides[half] * mine], axis=1))
            across = dot(jnp.concatenate(lefts, axis=0), right, NN)
            for m in range(32):
                along = t_ref[at(top + m), :] + t_ref[at(top + m + 2), :]
                s_ref[at(top + m), :] = (across[m * KP : (m + 1) * KP] + 0.125 * along) * root_ref[...]
            return 0

        lax.fori_loop(0, 2, rows, 0)
    s_ref[at(0), :] += 0.125 * north * root_ref[...]
    s_ref[at(N - 1), :] += 0.125 * south * root_ref[...]


def final_kernel(p0, p1, p2, p3, s_ref, lab_ref, gl_ref, w_ref, out_ref, e_ref):
    own = column(gl_ref[...].astype(F32), N) + jnp.zeros((N, N), F32)
    lefts, rights = [], []
    for p in (p0, p1, p2, p3):
        pay = p[...]
        gl = pay[LEV + 2 : LEV + 3].astype(F32) * 64.0 + pay[LEV + 3 : LEV + 4].astype(F32)
        lefts.append(pay)
        rights.append(jnp.where(own == gl, 1.0, 0.0).astype(BF16))
    total = dot(jnp.concatenate(lefts, axis=1), jnp.concatenate(rights, axis=1), NT)
    count = 256.0 * total[LEV : LEV + 1] + 32.0 * total[LEV + 1 : LEV + 2]
    root = jnp.sqrt(column(w_ref[...], KP))
    profile = root * (total / jnp.maximum(count, 1.0))
    energy = jnp.sum(profile * profile, axis=0, keepdims=True)
    row = iota((KP, N), 0)
    table = jnp.where(row == LEV, energy, profile)
    hi = table.astype(BF16)
    left = jnp.concatenate([hi, (table - hi.astype(F32)).astype(BF16)], axis=1)
    ids = iota((N, N), 0)

    def patch_row(q):
        mark = jnp.where(lab_ref[pl.ds(4 * q, 1), :] == ids, 1.0, 0.0).astype(BF16)
        placed = dot(left, jnp.concatenate([mark, mark], axis=0), NN)
        e = placed[LEV : LEV + 1]
        placed = jnp.where(row == LEV, 0.0, placed)
        for m in range(4):
            r = 4 * q + m
            d = s_ref[pl.ds(pl.multiple_of(r * KP, 8), KP), :] - placed
            out_ref[pl.ds(r, 1), :] = jnp.sum(d * d, axis=0, keepdims=True)
            e_ref[pl.ds(r, 1), :] = e

    def patch_rows(i, _):
        for m in range(16):
            patch_row(16 * i + m)
        return 0

    lax.fori_loop(0, N // 64, patch_rows, 0)
    out_ref[...] = jnp.sqrt(out_ref[...] / e_ref[...])


def params(mib):
    return pltpu.CompilerParams(vmem_limit_bytes=mib * 1024 * 1024)


def cost(flops, moved):
    return pl.CostEstimate(flops=flops, bytes_accessed=moved, transcendentals=0)


def shards(humidity, wind_u, wind_v, weights, labels, global_labels):
    vmem = pl.BlockSpec(memory_space=pltpu.VMEM)
    anywhere = pl.BlockSpec(memory_space=pl.ANY)
    edge = pltpu.VMEM((KP, N), BF16)
    gl = global_labels.reshape(1, N)
    w = weights.reshape(1, LEV)
    t, s0, s1, c0, c1 = pl.pallas_call(
        transport_kernel,
        out_shape=(pltpu.VMEM(((N + 2) * KP, N), F32), edge, edge, edge, edge),
        in_specs=[anywhere] * 3,
        out_specs=[vmem] * 5,
        scratch_shapes=[pltpu.VMEM((LEV, N, N), BF16)] * 3
        + [pltpu.VMEM((3, N, N), BF16), pltpu.SemaphoreType.DMA((len(CHUNKS), 3))],
        compiler_params=params(18),
        cost_estimate=cost(30_000_000, 23_000_000),
        name="transport",
    )(*(pltpu.with_memory_space_constraint(x, pltpu.HBM) for x in (humidity, wind_u, wind_v)))
    r1 = lax.ppermute(s1, "lat", [(i, (i + 1) % 8 if i % 2 else (i - 1) % 8) for i in range(8)])
    r0 = lax.ppermute(s0, "lat", [(i, i ^ 1) for i in range(8)])
    ro = lax.ppermute(c1, "lon", [(j, (j + 1) % 16 if j % 2 else (j - 1) % 16) for j in range(16)])
    rc = lax.ppermute(c0, "lon", [(j, j ^ 1) for j in range(16)])
    t0 = pl.pallas_call(
        sums_kernel,
        out_shape=pltpu.VMEM((KP, N), F32),
        in_specs=[vmem] * 2,
        out_specs=vmem,
        scratch_shapes=[pltpu.VMEM((N, N), jnp.int32)] * 2,
        compiler_params=params(8),
        cost_estimate=cost(600_000_000, 9_500_000),
        name="sums",
    )(t, labels)
    pay = pl.pallas_call(
        pack_kernel,
        out_shape=edge,
        in_specs=[vmem] * 7,
        out_specs=vmem,
        compiler_params=params(8),
        cost_estimate=cost(20_000_000, 300_000),
        name="pack",
    )(t0, r0, r1, rc, ro, labels, gl)
    p2 = lax.ppermute(pay, "lat", [(i, (i + 4) % 8) for i in range(8)])
    p1 = lax.ppermute(pay, "lon", [(j, j ^ 1) for j in range(16)])
    p3 = lax.ppermute(p2, "lon", [(j, j ^ 1) for j in range(16)])
    s = pl.pallas_call(
        smooth_kernel,
        out_shape=pltpu.VMEM((N * KP, N), F32),
        in_specs=[vmem] * 6,
        out_specs=vmem,
        scratch_shapes=[pltpu.VMEM((KP, N), F32)],
        compiler_params=params(16),
        cost_estimate=cost(1_200_000_000, 19_000_000),
        name="smooth",
    )(t, r0, r1, rc, ro, w)
    return pl.pallas_call(
        final_kernel,
        out_shape=jax.ShapeDtypeStruct((N, N), F32),
        in_specs=[vmem] * 8,
        out_specs=vmem,
        scratch_shapes=[pltpu.VMEM((N, N), F32)],
        compiler_params=params(8),
        cost_estimate=cost(300_000_000, 9_500_000),
        name="final",
    )(pay, p1, p2, p3, s, labels, gl, w)


def solution(mesh):
    return jax.shard_map(
        shards,
        mesh=mesh,
        in_specs=(
            P(None, "lat", "lon"),
            P(None, "lat", "lon"),
            P(None, "lat", "lon"),
            P(),
            P("lat", "lon"),
            P("lat", "lon", None),
        ),
        out_specs=P("lat", "lon"),
        check_vma=False,
    )
```

```python
import functools

import jax
import jax.numpy as jnp
from jax import lax
from jax.experimental import pallas as pl
from jax.experimental.pallas import tpu as pltpu
from jax.sharding import PartitionSpec as P

F32 = jnp.float32
BF16 = jnp.bfloat16
LEV = 137
KP = 152
N = 128
CHUNKS = ((0, 8), (8, 16), (24, 24), (48, 24), (72, 24), (96, 24), (120, 8), (128, 9))
NT = (((1,), (1,)), ((), ()))
NN = (((1,), (0,)), ((), ()))


def iota(shape, dim):
    return lax.broadcasted_iota(jnp.int32, shape, dim)


def dot(a, b, dims):
    return lax.dot_general(a, b, dims, preferred_element_type=F32)


def column(row, rows):
    shape = (rows, row.shape[1])
    return jnp.sum(jnp.where(iota(shape, 0) == iota(shape, 1), row, 0.0), axis=1, keepdims=True)


def ends():
    shape = (16, N)
    first = (iota(shape, 0) == 0) & (iota(shape, 1) == 0)
    last = (iota(shape, 0) == 1) & (iota(shape, 1) == N - 1)
    return jnp.where(first | last, 1.0, 0.0).astype(BF16)


def halos(r0, r1, rc, ro):
    i, j = lax.axis_index("lat"), lax.axis_index("lon")
    i_even, j_even = lax.rem(i, 2) == 0, lax.rem(j, 2) == 0
    r0, r1, rc, ro = (r[...].astype(F32) for r in (r0, r1, rc, ro))
    north = jnp.where(i == 0, 0.0, jnp.where(i_even, r1, r0))
    south = jnp.where(i == 7, 0.0, jnp.where(i_even, r0, r1))
    west = jnp.where(j_even, ro, rc)
    east = jnp.where(j_even, rc, ro)
    return north, south, west, east


def transport_kernel(h_hbm, u_hbm, v_hbm, t_ref, s0_ref, s1_ref, c0_ref, c1_ref, hb, ub, vb, cols, sems):
    copies = []
    for c, (a, n) in enumerate(CHUNKS):
        row = []
        for m, (src, dst) in enumerate(((h_hbm, hb), (u_hbm, ub), (v_hbm, vb))):
            copy = pltpu.make_async_copy(src.at[pl.ds(a, n)], dst.at[pl.ds(a, n)], sems.at[c, m])
            copy.start()
            row.append(copy)
        copies.append(row)
    zeros = jnp.zeros((N, N), F32)
    for k in range(LEV, KP):
        t_ref[pl.ds(KP + k, N, stride=KP), :] = zeros
    blank = jnp.zeros((KP, N), F32)
    t_ref[pl.ds(0, KP), :] = blank
    t_ref[pl.ds((N + 1) * KP, KP), :] = blank
    cols[...] = jnp.zeros((3, N, N), BF16)
    lane = iota((N, N), 1)

    def level(k):
        parts = []
        for b in range(0, N, 32):
            rows = pl.ds(b, 32)
            u, v = ub[k, rows, :], vb[k, rows, :]
            x = (u * u + v * v).astype(F32) + 1.0
            t = hb[k, rows, :].astype(F32) * (x * lax.rsqrt(x))
            t_ref[pl.ds((1 + b) * KP + k, 32, stride=KP), :] = t
            parts.append(t.astype(BF16))
        return jnp.concatenate(parts, axis=0)

    def group(k, size):
        ends = level(k)
        for q in range(1, size):
            moved = pltpu.roll(level(k + q), 2 * q, 1)
            ends = jnp.where((lane == 2 * q) | (lane == 2 * q - 1), moved, ends)
        shift = 2 * lax.rem(k, 64)
        mine = lax.rem(lane - shift + N + 1, N) < 2 * size
        block = lax.div(k, 64)
        cols[block] = jnp.where(mine, pltpu.roll(ends, shift, 1), cols[block])

    for (a, n), row in zip(CHUNKS, copies):
        for copy in row:
            copy.wait()

        def groups(g, _, a=a):
            group(a + 8 * g, 8)
            return 0

        lax.fori_loop(0, n // 8, groups, 0)
        if n % 8:
            group(a + n - n % 8, n % 8)
    i_even = lax.rem(lax.axis_index("lat"), 2) == 0
    j_even = lax.rem(lax.axis_index("lon"), 2) == 0

    def row_at(top):
        start = pl.multiple_of(jnp.where(top, KP, N * KP), 8)
        return t_ref[pl.ds(start, KP), :].astype(BF16)

    k, at = iota((KP, 3 * N), 0), iota((KP, 3 * N), 1)
    left_at = 2 * k
    right_at = jnp.where(lax.rem(k, 64) == 0, 2 * k + N - 1, 2 * k - 1)
    packed = jnp.concatenate([cols[0], cols[1], cols[2]], axis=1)

    def col_at(left):
        pick = jnp.where(at == jnp.where(left, left_at, right_at), 1.0, 0.0).astype(BF16)
        return dot(pick, packed, NT).astype(BF16)

    s0_ref[...] = row_at(jnp.logical_not(i_even))
    s1_ref[...] = row_at(i_even)
    c0_ref[...] = col_at(jnp.logical_not(j_even))
    c1_ref[...] = col_at(j_even)


def sums_kernel(t_ref, lab_ref, t0_ref, west_ref, east_ref):
    lab = lab_ref[...]
    lane = iota((N, N), 1)
    west_ref[...] = jnp.where(lane == 0, -1, pltpu.roll(lab, 1, 1))
    east_ref[...] = jnp.where(lane == N - 1, -1, pltpu.roll(lab, N - 1, 1))
    ids = iota((N, N), 0).astype(F32).astype(BF16)
    t0_ref[...] = jnp.zeros((KP, N), F32)
    last = iota((8, N), 0) + (LEV - LEV % 8)

    def patch_row(q):
        base = pl.multiple_of((1 + 4 * q) * KP, 8)
        x = [t_ref[pl.ds(base + m * KP, KP), :] for m in range(-1, 5)]
        whole = x[1] + x[2] + x[3] + x[4]
        step = (x[0] - x[4]) + (x[5] - x[1])
        step = jnp.concatenate([step[: LEV - LEV % 8], jnp.where(last == LEV, 32.0, step[LEV - LEV % 8 : KP - 8]), step[KP - 8 :]], axis=0)
        left = jnp.concatenate([whole.astype(BF16), step.astype(BF16)], axis=1)

        def marks(ref):
            row = ref[pl.ds(4 * q, 1), :].astype(F32).astype(BF16)
            return jnp.where(row == ids, BF16(0.125), BF16(0.0))

        here = marks(lab_ref)
        spread = here * BF16(6.0) + (marks(west_ref) + marks(east_ref))
        return left, jnp.concatenate([spread, here], axis=1)

    def patch_rows(i, _):
        pairs = [patch_row(16 * i + m) for m in range(16)]
        left, right = (jnp.concatenate(p, axis=1) for p in zip(*pairs))
        t0_ref[...] += dot(left, right, NT)
        return 0

    lax.fori_loop(0, N // 64, patch_rows, 0)


def pack_kernel(t0_ref, r0, r1, rc, ro, lab_ref, gl_ref, pay_ref):
    north, south, west, east = halos(r0, r1, rc, ro)
    lab = lab_ref[...].astype(F32)
    ids = iota((N, N), 0).astype(F32)
    sides = dot(ends(), lab.astype(BF16), NT)

    def marks(row):
        return jnp.where(row == ids, 0.125, 0.0)

    left = jnp.concatenate([north, south, west, east], axis=1).astype(BF16)
    right = jnp.concatenate(
        [marks(lab[0:1]), marks(lab[N - 1 : N]), marks(sides[0:1]), marks(sides[1:2])], axis=1
    ).astype(BF16)
    total = t0_ref[...] + dot(left, right, NT)
    count = total[LEV : LEV + 1] * (1.0 / 32.0)
    count_hi = jnp.floor(count * 0.125)
    gl = gl_ref[...].astype(F32)
    gl_hi = jnp.floor(gl * (1.0 / 64.0))
    row = iota((KP, N), 0)
    for m, extra in enumerate((count_hi, count - 8.0 * count_hi, gl_hi, gl - 64.0 * gl_hi)):
        total = jnp.where(row == LEV + m, extra, total)
    pay_ref[...] = total.astype(BF16)


def smooth_kernel(half, t_ref, r0, r1, rc, ro, w_ref, s_ref, root_ref):
    north, south, west, east = halos(r0, r1, rc, ro)
    low = iota((KP, N), 1) < 64
    if half == 0:
        side = jnp.where(low, west, pltpu.roll(east, 64, 1)).astype(BF16)
    else:
        side = jnp.where(low, pltpu.roll(west, 64, 1), east).astype(BF16)
    root_ref[...] = jnp.sqrt(column(w_ref[...], KP)) * 0.125 + jnp.zeros((KP, N), F32)
    a, c = iota((2 * N, N), 0), iota((2 * N, N), 1)
    band = jnp.where(a == c, 4.0, jnp.where(jnp.abs(a - c) == 1, 1.0, 0.0))
    edge = jnp.where(c == jnp.where(a < N + 64, 0, N - 1), 1.0, 0.0)
    right = jnp.where(a < N, band, edge).astype(BF16)
    lane = lax.rem(iota((1, N), 1), 64)

    def at(r):
        return pl.ds(pl.multiple_of(r * KP, 8), KP)

    def rows(i, _):
        top = 64 * half + 32 * i
        lefts = []
        for m in range(32):
            mine = jnp.where(lane == 32 * i + m, 1.0, 0.0).astype(BF16)
            lefts.append(jnp.concatenate([t_ref[at(top + m + 1), :].astype(BF16), side * mine], axis=1))
        across = dot(jnp.concatenate(lefts, axis=0), right, NN)
        for m in range(32):
            along = t_ref[at(top + m), :] + t_ref[at(top + m + 2), :]
            s_ref[at(32 * i + m), :] = (across[m * KP : (m + 1) * KP] + along) * root_ref[...]
        return 0

    lax.fori_loop(0, 2, rows, 0)
    if half == 0:
        s_ref[at(0), :] += north * root_ref[...]
    else:
        s_ref[at(63), :] += south * root_ref[...]


def final_kernel(p0, p1, p2, p3, s0_ref, s1_ref, lab_ref, gl_ref, w_ref, out_ref, e_ref):
    own = column(gl_ref[...].astype(F32), N) + jnp.zeros((N, N), F32)
    lefts, rights = [], []
    for p in (p0, p1, p2, p3):
        pay = p[...]
        gl = pay[LEV + 2 : LEV + 3].astype(F32) * 64.0 + pay[LEV + 3 : LEV + 4].astype(F32)
        lefts.append(pay)
        rights.append(jnp.where(own == gl, 1.0, 0.0).astype(BF16))
    total = dot(jnp.concatenate(lefts, axis=1), jnp.concatenate(rights, axis=1), NT)
    count = 256.0 * total[LEV : LEV + 1] + 32.0 * total[LEV + 1 : LEV + 2]
    root = jnp.sqrt(column(w_ref[...], KP))
    profile = root * (total / jnp.maximum(count, 1.0))
    energy = jnp.sum(profile * profile, axis=0, keepdims=True)
    table = jnp.where(iota((KP, N), 0) == LEV, energy, profile)
    hi = table.astype(BF16)
    left = jnp.concatenate([hi, (table - hi.astype(F32)).astype(BF16)], axis=1)
    ids = iota((N, N), 0).astype(F32).astype(BF16)
    base = LEV - LEV % 8
    inside = iota((8, N), 0) + base < LEV

    def patch_row(q, s_ref, top):
        row = lab_ref[pl.ds(4 * q, 1), :].astype(F32).astype(BF16)
        mark = jnp.where(row == ids, BF16(1.0), BF16(0.0))
        placed = dot(left, jnp.concatenate([mark, mark], axis=0), NN)
        e = placed[LEV : LEV + 1]
        placed = jnp.concatenate([placed[:base], jnp.where(inside, placed[base : base + 8], 0.0)], axis=0)
        for m in range(4):
            r = 4 * q + m
            d = s_ref[pl.ds((r - top) * KP, base + 8), :] - placed
            out_ref[pl.ds(r, 1), :] = jnp.sum(d * d, axis=0, keepdims=True)
            e_ref[pl.ds(r, 1), :] = e

    for half, s_ref in enumerate((s0_ref, s1_ref)):
        for q in range(16 * half, 16 * half + 16):
            patch_row(q, s_ref, 64 * half)
    out_ref[...] = jnp.sqrt(out_ref[...] / e_ref[...])


def outer(i, j):
    if i in (0, 7):
        return 16 * i + (j ^ 1)
    return 16 * (i + 1 if i % 2 else i - 1) + j


def params(mib):
    return pltpu.CompilerParams(vmem_limit_bytes=mib * 1024 * 1024)


def cost(flops, moved):
    return pl.CostEstimate(flops=flops, bytes_accessed=moved, transcendentals=0)


def shards(humidity, wind_u, wind_v, weights, labels, global_labels):
    vmem = pl.BlockSpec(memory_space=pltpu.VMEM)
    anywhere = pl.BlockSpec(memory_space=pl.ANY)
    edge = pltpu.VMEM((KP, N), BF16)
    gl = global_labels.reshape(1, N)
    w = weights.reshape(1, LEV)
    t, s0, s1, c0, c1 = pl.pallas_call(
        transport_kernel,
        out_shape=(pltpu.VMEM(((N + 2) * KP, N), F32), edge, edge, edge, edge),
        in_specs=[anywhere] * 3,
        out_specs=[vmem] * 5,
        scratch_shapes=[pltpu.VMEM((LEV, N, N), BF16)] * 3
        + [pltpu.VMEM((3, N, N), BF16), pltpu.SemaphoreType.DMA((len(CHUNKS), 3))],
        compiler_params=params(18),
        cost_estimate=cost(30_000_000, 23_000_000),
        name="transport",
    )(*(pltpu.with_memory_space_constraint(x, pltpu.HBM) for x in (humidity, wind_u, wind_v)))
    r1 = lax.ppermute(s1, ("lat", "lon"), [(16 * i + j, outer(i, j)) for i in range(8) for j in range(16)])
    r0 = lax.ppermute(s0, "lat", [(i, i ^ 1) for i in range(8)])
    ro = lax.ppermute(c1, "lon", [(j, (j + 1) % 16 if j % 2 else (j - 1) % 16) for j in range(16)])
    rc = lax.ppermute(c0, "lon", [(j, j ^ 1) for j in range(16)])
    t0 = pl.pallas_call(
        sums_kernel,
        out_shape=pltpu.VMEM((KP, N), F32),
        in_specs=[vmem] * 2,
        out_specs=vmem,
        scratch_shapes=[pltpu.VMEM((N, N), jnp.int32)] * 2,
        compiler_params=params(8),
        cost_estimate=cost(600_000_000, 9_500_000),
        name="sums",
    )(t, labels)
    pay = pl.pallas_call(
        pack_kernel,
        out_shape=edge,
        in_specs=[vmem] * 7,
        out_specs=vmem,
        compiler_params=params(8),
        cost_estimate=cost(20_000_000, 300_000),
        name="pack",
    )(t0, r0, r1, rc, ro, labels, gl)
    p2 = lax.ppermute(pay, "lat", [(i, (i + 4) % 8) for i in range(8)])
    p1 = lax.ppermute(pay, "lon", [(j, j ^ 1) for j in range(16)])
    p3 = lax.ppermute(p2, "lon", [(j, j ^ 1) for j in range(16)])
    s0, s1 = (
        pl.pallas_call(
            functools.partial(smooth_kernel, half),
            out_shape=pltpu.VMEM((N // 2 * KP, N), F32),
            in_specs=[vmem] * 6,
            out_specs=vmem,
            scratch_shapes=[pltpu.VMEM((KP, N), F32)],
            compiler_params=params(12),
            cost_estimate=cost(600_000_000, 9_500_000),
            name="smooth",
        )(t, r0, r1, rc, ro, w)
        for half in range(2)
    )
    return pl.pallas_call(
        final_kernel,
        out_shape=jax.ShapeDtypeStruct((N, N), F32),
        in_specs=[vmem] * 9,
        out_specs=vmem,
        scratch_shapes=[pltpu.VMEM((N, N), F32)],
        compiler_params=params(8),
        cost_estimate=cost(300_000_000, 9_500_000),
        name="final",
    )(pay, p1, p2, p3, s0, s1, labels, gl, w)


def solution(mesh):
    return jax.shard_map(
        shards,
        mesh=mesh,
        in_specs=(
            P(None, "lat", "lon"),
            P(None, "lat", "lon"),
            P(None, "lat", "lon"),
            P(),
            P("lat", "lon"),
            P("lat", "lon", None),
        ),
        out_specs=P("lat", "lon"),
        check_vma=False,
    )
```

```python
import functools

import jax
import jax.numpy as jnp
from jax import lax
from jax.experimental import pallas as pl
from jax.experimental.pallas import tpu as pltpu
from jax.sharding import PartitionSpec as P

F32 = jnp.float32
BF16 = jnp.bfloat16
LEV = 137
KA = 144
KP = 152
N = 128
CHUNKS = ((0, 8), (8, 16), (24, 24), (48, 24), (72, 24), (96, 24), (120, 8), (128, 9))
NT = (((1,), (1,)), ((), ()))
NN = (((1,), (0,)), ((), ()))


def iota(shape, dim):
    return lax.broadcasted_iota(jnp.int32, shape, dim)


def dot(a, b, dims):
    return lax.dot_general(a, b, dims, preferred_element_type=F32)


def column(row, rows):
    shape = (rows, row.shape[1])
    return jnp.sum(jnp.where(iota(shape, 0) == iota(shape, 1), row, 0.0), axis=1, keepdims=True)


def ends():
    shape = (16, N)
    first = (iota(shape, 0) == 0) & (iota(shape, 1) == 0)
    last = (iota(shape, 0) == 1) & (iota(shape, 1) == N - 1)
    return jnp.where(first | last, 1.0, 0.0).astype(BF16)


def halos(r0, r1, rc, ro):
    i, j = lax.axis_index("lat"), lax.axis_index("lon")
    i_even, j_even = lax.rem(i, 2) == 0, lax.rem(j, 2) == 0
    r0, r1, rc, ro = (r[...].astype(F32) for r in (r0, r1, rc, ro))
    north = jnp.where(i == 0, 0.0, jnp.where(i_even, r1, r0))
    south = jnp.where(i == 7, 0.0, jnp.where(i_even, r0, r1))
    west = jnp.where(j_even, ro, rc)
    east = jnp.where(j_even, rc, ro)
    return north, south, west, east


def transport_kernel(h_hbm, u_hbm, v_hbm, t_ref, s0_ref, s1_ref, c0_ref, c1_ref, hb, ub, vb, cols, near, picks, sems):
    copies = []
    for c, (a, n) in enumerate(CHUNKS):
        row = []
        for m, (src, dst) in enumerate(((h_hbm, hb), (u_hbm, ub), (v_hbm, vb))):
            copy = pltpu.make_async_copy(src.at[pl.ds(a, n)], dst.at[pl.ds(a, n)], sems.at[c, m])
            copy.start()
            row.append(copy)
        copies.append(row)
    zeros = jnp.zeros((N, N), F32)
    for k in range(LEV, KA):
        t_ref[pl.ds(KP + k, N, stride=KP), :] = zeros
    blank = jnp.zeros((KA, N), F32)
    t_ref[pl.ds(0, KA), :] = blank
    t_ref[pl.ds((N + 1) * KP, KA), :] = blank
    cols[...] = jnp.zeros((3, N, N), BF16)
    lane = iota((N, N), 1)
    i_even = lax.rem(lax.axis_index("lat"), 2) == 0
    j_even = lax.rem(lax.axis_index("lon"), 2) == 0
    k, at = iota((KA, 3 * N), 0), iota((KA, 3 * N), 1)
    left_at = 2 * k
    right_at = jnp.where(lax.rem(k, 64) == 0, 2 * k + N - 1, 2 * k - 1)
    picks[0] = jnp.where(at == jnp.where(j_even, right_at, left_at), 1.0, 0.0).astype(BF16)
    picks[1] = jnp.where(at == jnp.where(j_even, left_at, right_at), 1.0, 0.0).astype(BF16)

    def level(k):
        parts = []
        for b in range(0, N, 32):
            rows = pl.ds(b, 32)
            u, v = ub[k, rows, :], vb[k, rows, :]
            x = (u * u + v * v).astype(F32) + 1.0
            t = hb[k, rows, :].astype(F32) * (x * lax.rsqrt(x))
            t_ref[pl.ds((1 + b) * KP + k, 32, stride=KP), :] = t
            parts.append(t.astype(BF16))
        return jnp.concatenate(parts, axis=0)

    def group(k, size):
        ends = level(k)
        for q in range(1, size):
            moved = pltpu.roll(level(k + q), 2 * q, 1)
            ends = jnp.where((lane == 2 * q) | (lane == 2 * q - 1), moved, ends)
        near[...] = ends

    def merge(k, size):
        shift = 2 * lax.rem(k, 64)
        mine = lax.rem(lane - shift + N + 1, N) < 2 * size
        block = lax.div(k, 64)
        cols[block] = jnp.where(mine, pltpu.roll(near[...], shift, 1), cols[block])

    for (a, n), row in zip(CHUNKS, copies):
        for copy in row:
            copy.wait()

        def groups(g, _, a=a):
            merge(a + 8 * g - 8, 8)
            group(a + 8 * g, 8)
            return 0

        if a == 0:
            group(0, 8)
        lax.fori_loop(1 if a == 0 else 0, n // 8, groups, 0)
        if n % 8:
            end = a + n - n % 8
            merge(end - 8, 8)
            group(end, n % 8)
            merge(end, n % 8)

    def row_at(top):
        start = pl.multiple_of(jnp.where(top, KP, N * KP), 8)
        return t_ref[pl.ds(start, KA), :].astype(BF16)

    packed = jnp.concatenate([cols[0], cols[1], cols[2]], axis=1)
    s0_ref[...] = row_at(jnp.logical_not(i_even))
    s1_ref[...] = row_at(i_even)
    c0_ref[...] = dot(picks[0], packed, NT).astype(BF16)
    c1_ref[...] = dot(picks[1], packed, NT).astype(BF16)


def sums_kernel(t_ref, lab_ref, gl_ref, w_ref, t0_ref, root_ref, own_ref, west_ref, east_ref):
    root_ref[...] = jnp.sqrt(column(w_ref[...], KA)) * 0.125 + jnp.zeros((KA, N), F32)
    own_ref[...] = column(gl_ref[...].astype(F32), N) + jnp.zeros((N, N), F32)
    lab = lab_ref[...]
    lane = iota((N, N), 1)
    west_ref[...] = jnp.where(lane == 0, -1, pltpu.roll(lab, 1, 1))
    east_ref[...] = jnp.where(lane == N - 1, -1, pltpu.roll(lab, N - 1, 1))
    ids = iota((N, N), 0).astype(F32).astype(BF16)
    t0_ref[...] = jnp.zeros((KA, N), F32)
    last = iota((8, N), 0) + (LEV - LEV % 8)

    def patch_row(q):
        base = pl.multiple_of((1 + 4 * q) * KP, 8)
        x = [t_ref[pl.ds(base + m * KP, KA), :] for m in range(-1, 5)]
        whole = x[1] + x[2] + x[3] + x[4]
        step = (x[0] - x[4]) + (x[5] - x[1])
        step = jnp.concatenate([step[: LEV - LEV % 8], jnp.where(last == LEV, 32.0, step[LEV - LEV % 8 :])], axis=0)
        left = jnp.concatenate([whole.astype(BF16), step.astype(BF16)], axis=1)

        def marks(ref):
            row = ref[pl.ds(4 * q, 1), :].astype(F32).astype(BF16)
            return jnp.where(row == ids, BF16(0.125), BF16(0.0))

        here = marks(lab_ref)
        spread = here * BF16(6.0) + (marks(west_ref) + marks(east_ref))
        return left, jnp.concatenate([spread, here], axis=1)

    def patch_rows(i, _):
        pairs = [patch_row(16 * i + m) for m in range(16)]
        left, right = (jnp.concatenate(p, axis=1) for p in zip(*pairs))
        t0_ref[...] += dot(left, right, NT)
        return 0

    lax.fori_loop(0, N // 64, patch_rows, 0)


def pack_kernel(t0_ref, r0, r1, rc, ro, lab_ref, gl_ref, pay_ref):
    north, south, west, east = halos(r0, r1, rc, ro)
    lab = lab_ref[...].astype(F32)
    ids = iota((N, N), 0).astype(F32)
    sides = dot(ends(), lab.astype(BF16), NT)

    def marks(row):
        return jnp.where(row == ids, 0.125, 0.0)

    left = jnp.concatenate([north, south, west, east], axis=1).astype(BF16)
    right = jnp.concatenate(
        [marks(lab[0:1]), marks(lab[N - 1 : N]), marks(sides[0:1]), marks(sides[1:2])], axis=1
    ).astype(BF16)
    total = t0_ref[...] + dot(left, right, NT)
    count = total[LEV : LEV + 1] * (1.0 / 32.0)
    count_hi = jnp.floor(count * 0.125)
    gl = gl_ref[...].astype(F32)
    gl_hi = jnp.floor(gl * (1.0 / 64.0))
    row = iota((KA, N), 0)
    for m, extra in enumerate((count_hi, count - 8.0 * count_hi, gl_hi, gl - 64.0 * gl_hi)):
        total = jnp.where(row == LEV + m, extra, total)
    pay_ref[...] = total.astype(BF16)


def smooth_kernel(half, t_ref, r0, r1, rc, ro, root_ref, s_ref, square_ref):
    north, south, west, east = halos(r0, r1, rc, ro)
    low = iota((KA, N), 1) < 64
    if half == 0:
        outside, side = north, jnp.where(low, west, pltpu.roll(east, 64, 1)).astype(BF16)
    else:
        outside, side = south, jnp.where(low, pltpu.roll(west, 64, 1), east).astype(BF16)
    a, c = iota((2 * N, N), 0), iota((2 * N, N), 1)
    band = jnp.where(a == c, 4.0, jnp.where(jnp.abs(a - c) == 1, 1.0, 0.0))
    edge = jnp.where(c == jnp.where(a < N + 64, 0, N - 1), 1.0, 0.0)
    right = jnp.where(a < N, band, edge).astype(BF16)
    lane = lax.rem(iota((1, N), 1), 64)

    def at(r):
        return pl.ds(pl.multiple_of(r * KP, 8), KA)

    def to(r):
        return pl.ds(pl.multiple_of(r * KA, 8), KA)

    def rows(i, _):
        top = 64 * half + 32 * i
        lefts = []
        for m in range(32):
            mine = jnp.where(lane == 32 * i + m, 1.0, 0.0).astype(BF16)
            lefts.append(jnp.concatenate([t_ref[at(top + m + 1), :].astype(BF16), side * mine], axis=1))
        across = dot(jnp.concatenate(lefts, axis=0), right, NN)
        for m in range(32):
            along = t_ref[at(top + m), :] + t_ref[at(top + m + 2), :]
            if m == (0 if half == 0 else 31):
                along = along + jnp.where(i == half, outside, 0.0)
            s = (across[m * KA : (m + 1) * KA] + along) * root_ref[...]
            s_ref[to(32 * i + m), :] = s
            square_ref[pl.ds(32 * i + m, 1), :] = jnp.sum(s * s, axis=0, keepdims=True)
        return 0

    lax.fori_loop(0, 2, rows, 0)


def final_kernel(p0, p1, p2, p3, s0_ref, s1_ref, square0, square1, lab_ref, own_ref, root_ref, out_ref, e_ref):
    own = own_ref[...]
    lefts, rights = [], []
    for p in (p0, p1, p2, p3):
        pay = p[...]
        gl = pay[LEV + 2 : LEV + 3].astype(F32) * 64.0 + pay[LEV + 3 : LEV + 4].astype(F32)
        lefts.append(pay)
        rights.append(jnp.where(own == gl, 1.0, 0.0).astype(BF16))
    total = dot(jnp.concatenate(lefts, axis=1), jnp.concatenate(rights, axis=1), NT)
    count = 256.0 * total[LEV : LEV + 1] + 32.0 * total[LEV + 1 : LEV + 2]
    profile = root_ref[...] * (total * (8.0 / jnp.maximum(count, 1.0)))
    hi = profile.astype(BF16).astype(F32)
    lo = (profile - hi).astype(BF16).astype(F32)
    profile = hi + lo
    energy = jnp.sum(profile * profile, axis=0, keepdims=True)
    energy_hi = energy.astype(BF16).astype(F32)
    row = iota((KA, N), 0)
    hi = jnp.where(row == LEV, energy_hi, hi).astype(BF16)
    lo = jnp.where(row == LEV, energy - energy_hi, lo).astype(BF16)
    left = jnp.concatenate([hi, lo], axis=1)
    ids = iota((N, N), 0).astype(F32).astype(BF16)

    def patch_row(q, s_ref, top):
        row = lab_ref[pl.ds(4 * q, 1), :].astype(F32).astype(BF16)
        mark = jnp.where(row == ids, BF16(1.0), BF16(0.0))
        placed = dot(left, jnp.concatenate([mark, mark], axis=0), NN)
        e_ref[pl.ds(4 * q, 4), :] = placed[LEV : LEV + 1] + jnp.zeros((4, N), F32)
        for m in range(4):
            r = 4 * q + m
            cross = s_ref[pl.ds((r - top) * KA, KA), :] * placed
            out_ref[pl.ds(r, 1), :] = jnp.sum(cross, axis=0, keepdims=True)

    for half, s_ref in enumerate((s0_ref, s1_ref)):
        for q in range(16 * half, 16 * half + 16):
            patch_row(q, s_ref, 64 * half)
    e = e_ref[...]
    square = jnp.concatenate([square0[...], square1[...]], axis=0)
    out_ref[...] = jnp.sqrt(jnp.maximum(square - 2.0 * out_ref[...] + e, 0.0) / e)


def outer(i, j):
    if i in (0, 7):
        return 16 * i + (j ^ 1)
    return 16 * (i + 1 if i % 2 else i - 1) + j


def params(mib):
    return pltpu.CompilerParams(vmem_limit_bytes=mib * 1024 * 1024)


def cost(flops, moved):
    return pl.CostEstimate(flops=flops, bytes_accessed=moved, transcendentals=0)


def shards(humidity, wind_u, wind_v, weights, labels, global_labels):
    vmem = pl.BlockSpec(memory_space=pltpu.VMEM)
    anywhere = pl.BlockSpec(memory_space=pl.ANY)
    edge = pltpu.VMEM((KA, N), BF16)
    gl = global_labels.reshape(1, N)
    w = weights.reshape(1, LEV)
    t, s0, s1, c0, c1 = pl.pallas_call(
        transport_kernel,
        out_shape=(pltpu.VMEM(((N + 2) * KP, N), F32), edge, edge, edge, edge),
        in_specs=[anywhere] * 3,
        out_specs=[vmem] * 5,
        scratch_shapes=[pltpu.VMEM((LEV, N, N), BF16)] * 3
        + [pltpu.VMEM((3, N, N), BF16), pltpu.VMEM((N, N), BF16), pltpu.VMEM((2, KA, 3 * N), BF16)]
        + [pltpu.SemaphoreType.DMA((len(CHUNKS), 3))],
        compiler_params=params(18),
        cost_estimate=cost(30_000_000, 23_000_000),
        name="transport",
    )(*(pltpu.with_memory_space_constraint(x, pltpu.HBM) for x in (humidity, wind_u, wind_v)))
    r1 = lax.ppermute(s1, ("lat", "lon"), [(16 * i + j, outer(i, j)) for i in range(8) for j in range(16)])
    r0 = lax.ppermute(s0, "lat", [(i, i ^ 1) for i in range(8)])
    ro = lax.ppermute(c1, "lon", [(j, (j + 1) % 16 if j % 2 else (j - 1) % 16) for j in range(16)])
    rc = lax.ppermute(c0, "lon", [(j, j ^ 1) for j in range(16)])
    t0, root, own = pl.pallas_call(
        sums_kernel,
        out_shape=(pltpu.VMEM((KA, N), F32), pltpu.VMEM((KA, N), F32), pltpu.VMEM((N, N), F32)),
        in_specs=[vmem] * 4,
        out_specs=[vmem] * 3,
        scratch_shapes=[pltpu.VMEM((N, N), jnp.int32)] * 2,
        compiler_params=params(8),
        cost_estimate=cost(600_000_000, 9_500_000),
        name="sums",
    )(t, labels, gl, w)
    pay = pl.pallas_call(
        pack_kernel,
        out_shape=edge,
        in_specs=[vmem] * 7,
        out_specs=vmem,
        compiler_params=params(8),
        cost_estimate=cost(20_000_000, 300_000),
        name="pack",
    )(t0, r0, r1, rc, ro, labels, gl)
    p2 = lax.ppermute(pay, "lat", [(i, (i + 4) % 8) for i in range(8)])
    p1 = lax.ppermute(pay, "lon", [(j, j ^ 1) for j in range(16)])
    p3 = lax.ppermute(p2, "lon", [(j, j ^ 1) for j in range(16)])
    (s0, square0), (s1, square1) = (
        pl.pallas_call(
            functools.partial(smooth_kernel, half),
            out_shape=(pltpu.VMEM((N // 2 * KA, N), F32), pltpu.VMEM((N // 2, N), F32)),
            in_specs=[vmem] * 6,
            out_specs=[vmem] * 2,
            compiler_params=params(12),
            cost_estimate=cost(600_000_000, 9_500_000),
            name="smooth",
        )(t, r0, r1, rc, ro, root)
        for half in range(2)
    )
    return pl.pallas_call(
        final_kernel,
        out_shape=jax.ShapeDtypeStruct((N, N), F32),
        in_specs=[vmem] * 11,
        out_specs=vmem,
        scratch_shapes=[pltpu.VMEM((N, N), F32)],
        compiler_params=params(8),
        cost_estimate=cost(300_000_000, 9_500_000),
        name="final",
    )(pay, p1, p2, p3, s0, s1, square0, square1, labels, own, root)


def solution(mesh):
    return jax.shard_map(
        shards,
        mesh=mesh,
        in_specs=(
            P(None, "lat", "lon"),
            P(None, "lat", "lon"),
            P(None, "lat", "lon"),
            P(),
            P("lat", "lon"),
            P("lat", "lon", None),
        ),
        out_specs=P("lat", "lon"),
        check_vma=False,
    )
```

```python
import jax
import jax.numpy as jnp
from jax import lax
from jax.experimental import pallas as pl
from jax.experimental.pallas import tpu as pltpu
from jax.sharding import PartitionSpec as P

F32 = jnp.float32
BF16 = jnp.bfloat16
LEV = 137
KA = 144
TOP = 88
KP = 152
N = 128
CHUNKS = ((0, 8), (8, 16), (24, 24), (48, 24), (72, 24), (96, 24), (120, 8), (128, 9))
NT = (((1,), (1,)), ((), ()))
NN = (((1,), (0,)), ((), ()))


def iota(shape, dim):
    return lax.broadcasted_iota(jnp.int32, shape, dim)


def dot(a, b, dims):
    return lax.dot_general(a, b, dims, preferred_element_type=F32)


def column(row, rows):
    shape = (rows, row.shape[1])
    return jnp.sum(jnp.where(iota(shape, 0) == iota(shape, 1), row, 0.0), axis=1, keepdims=True)


def ends():
    shape = (16, N)
    first = (iota(shape, 0) == 0) & (iota(shape, 1) == 0)
    last = (iota(shape, 0) == 1) & (iota(shape, 1) == N - 1)
    return jnp.where(first | last, 1.0, 0.0).astype(BF16)


def north_first():
    i, j = lax.axis_index("lat"), lax.axis_index("lon")
    return (lax.rem(i, 2) == 0) == (lax.rem(j, 4) < 2)


def halos(r0, r1, rc, ro):
    i, j = lax.axis_index("lat"), lax.axis_index("lon")
    first, j_even = north_first(), lax.rem(j, 2) == 0
    r0, r1, rc, ro = (r[...].astype(F32) for r in (r0, r1, rc, ro))
    north = jnp.where(i == 0, 0.0, jnp.where(first, r0, r1))
    south = jnp.where(i == 7, 0.0, jnp.where(first, r1, r0))
    west = jnp.where(j_even, ro, rc)
    east = jnp.where(j_even, rc, ro)
    return north, south, west, east


def transport_kernel(h_hbm, u_hbm, v_hbm, t_ref, s0_ref, s1_ref, c0_ref, c1_ref, hb, ub, vb, cols, near, picks, sems):
    copies = []
    for c, (a, n) in enumerate(CHUNKS):
        row = []
        for m, (src, dst) in enumerate(((h_hbm, hb), (u_hbm, ub), (v_hbm, vb))):
            copy = pltpu.make_async_copy(src.at[pl.ds(a, n)], dst.at[pl.ds(a, n)], sems.at[c, m])
            copy.start()
            row.append(copy)
        copies.append(row)
    zeros = jnp.zeros((N, N), F32)
    for k in range(LEV, KA):
        t_ref[pl.ds(KP + k, N, stride=KP), :] = zeros
    blank = jnp.zeros((KA, N), F32)
    t_ref[pl.ds(0, KA), :] = blank
    t_ref[pl.ds((N + 1) * KP, KA), :] = blank
    cols[...] = jnp.zeros((3, N, N), BF16)
    lane = iota((N, N), 1)
    first, j_even = north_first(), lax.rem(lax.axis_index("lon"), 2) == 0
    k, at = iota((KA, 3 * N), 0), iota((KA, 3 * N), 1)
    left_at = 2 * k
    right_at = jnp.where(lax.rem(k, 64) == 0, 2 * k + N - 1, 2 * k - 1)
    picks[0] = jnp.where(at == jnp.where(j_even, right_at, left_at), 1.0, 0.0).astype(BF16)
    picks[1] = jnp.where(at == jnp.where(j_even, left_at, right_at), 1.0, 0.0).astype(BF16)

    def level(k):
        parts = []
        for b in range(0, N, 32):
            rows = pl.ds(b, 32)
            u, v = ub[k, rows, :], vb[k, rows, :]
            x = (u * u + v * v).astype(F32) + 1.0
            t = hb[k, rows, :].astype(F32) * (x * lax.rsqrt(x))
            t_ref[pl.ds((1 + b) * KP + k, 32, stride=KP), :] = t
            parts.append(t.astype(BF16))
        return jnp.concatenate(parts, axis=0)

    def group(k, size):
        ends = level(k)
        for q in range(1, size):
            moved = pltpu.roll(level(k + q), 2 * q, 1)
            ends = jnp.where((lane == 2 * q) | (lane == 2 * q - 1), moved, ends)
        near[...] = ends

    def merge(k, size):
        shift = 2 * lax.rem(k, 64)
        mine = lax.rem(lane - shift + N + 1, N) < 2 * size
        block = lax.div(k, 64)
        cols[block] = jnp.where(mine, pltpu.roll(near[...], shift, 1), cols[block])

    for (a, n), row in zip(CHUNKS, copies):
        for copy in row:
            copy.wait()

        def groups(g, _, a=a):
            merge(a + 8 * g - 8, 8)
            group(a + 8 * g, 8)
            return 0

        if a == 0:
            group(0, 8)
        lax.fori_loop(1 if a == 0 else 0, n // 8, groups, 0)
        if n % 8:
            end = a + n - n % 8
            merge(end - 8, 8)
            group(end, n % 8)
            merge(end, n % 8)

    def row_at(top):
        start = pl.multiple_of(jnp.where(top, KP, N * KP), 8)
        return t_ref[pl.ds(start, KA), :].astype(BF16)

    packed = jnp.concatenate([cols[0], cols[1], cols[2]], axis=1)
    s0_ref[...] = row_at(first)
    s1_ref[...] = row_at(jnp.logical_not(first))
    c0_ref[...] = dot(picks[0], packed, NT).astype(BF16)
    c1_ref[...] = dot(picks[1], packed, NT).astype(BF16)


def sums_kernel(t_ref, lab_ref, gl_ref, w_ref, t0_ref, root_ref, own_ref, band_ref, west_ref, east_ref):
    root_ref[...] = jnp.sqrt(column(w_ref[...], KA)) * 0.125 + jnp.zeros((KA, N), F32)
    own_ref[...] = column(gl_ref[...].astype(F32), N) + jnp.zeros((N, N), F32)
    a, c = iota((2 * N, N), 0), iota((2 * N, N), 1)
    band = jnp.where(a == c, 4.0, jnp.where(jnp.abs(a - c) == 1, 1.0, 0.0))
    edge = jnp.where(c == jnp.where(a < N + 64, 0, N - 1), 1.0, 0.0)
    band_ref[...] = jnp.where(a < N, band, edge).astype(BF16)
    lab = lab_ref[...]
    lane = iota((N, N), 1)
    west_ref[...] = jnp.where(lane == 0, -1, pltpu.roll(lab, 1, 1))
    east_ref[...] = jnp.where(lane == N - 1, -1, pltpu.roll(lab, N - 1, 1))
    ids = iota((N, N), 0).astype(F32).astype(BF16)
    t0_ref[...] = jnp.zeros((KA, N), F32)
    last = iota((8, N), 0) + (LEV - LEV % 8)

    def patch_row(q):
        base = pl.multiple_of((1 + 4 * q) * KP, 8)
        x = [t_ref[pl.ds(base + m * KP, KA), :] for m in range(-1, 5)]
        whole = x[1] + x[2] + x[3] + x[4]
        step = (x[0] - x[4]) + (x[5] - x[1])
        step = jnp.concatenate([step[: LEV - LEV % 8], jnp.where(last == LEV, 32.0, step[LEV - LEV % 8 :])], axis=0)
        left = jnp.concatenate([whole.astype(BF16), step.astype(BF16)], axis=1)

        def marks(ref):
            row = ref[pl.ds(4 * q, 1), :].astype(F32).astype(BF16)
            return jnp.where(row == ids, BF16(0.125), BF16(0.0))

        here = marks(lab_ref)
        spread = here * BF16(6.0) + (marks(west_ref) + marks(east_ref))
        return left, jnp.concatenate([spread, here], axis=1)

    def patch_rows(i, _):
        pairs = [patch_row(16 * i + m) for m in range(16)]
        left, right = (jnp.concatenate(p, axis=1) for p in zip(*pairs))
        t0_ref[...] += dot(left, right, NT)
        return 0

    lax.fori_loop(0, N // 64, patch_rows, 0)


def pack_kernel(t0_ref, r0, r1, ro, rc, lab_ref, gl_ref, pay_ref):
    north, south, west, east = halos(r0, r1, rc, ro)
    lab = lab_ref[...].astype(F32)
    ids = iota((N, N), 0).astype(F32)
    sides = dot(ends(), lab.astype(BF16), NT)

    def marks(row):
        return jnp.where(row == ids, 0.125, 0.0)

    left = jnp.concatenate([north, south, west, east], axis=1).astype(BF16)
    right = jnp.concatenate(
        [marks(lab[0:1]), marks(lab[N - 1 : N]), marks(sides[0:1]), marks(sides[1:2])], axis=1
    ).astype(BF16)
    total = t0_ref[...] + dot(left, right, NT)
    count = total[LEV : LEV + 1] * (1.0 / 32.0)
    count_hi = jnp.floor(count * 0.125)
    gl = gl_ref[...].astype(F32)
    gl_hi = jnp.floor(gl * (1.0 / 64.0))
    row = iota((KA, N), 0)
    for m, extra in enumerate((count_hi, count - 8.0 * count_hi, gl_hi, gl - 64.0 * gl_hi)):
        total = jnp.where(row == LEV + m, extra, total)
    pay_ref[...] = total.astype(BF16)


def smooth_rows(t_ref, side, root_ref, band_ref, s_ref, square_ref, row, count, to, extra=None):
    lane = lax.rem(iota((1, N), 1), 64)

    def at(r):
        return pl.ds(pl.multiple_of(r * KP, 8), KA)

    lefts = []
    for m in range(count):
        mine = jnp.where(lane == lax.rem(row + m, 64), 1.0, 0.0).astype(BF16)
        lefts.append(jnp.concatenate([t_ref[at(row + m + 1), :].astype(BF16), side * mine], axis=1))
    across = dot(jnp.concatenate(lefts, axis=0), band_ref[...], NN)
    for m in range(count):
        along = t_ref[at(row + m), :] + t_ref[at(row + m + 2), :]
        if extra is not None and m == extra[0]:
            along = along + extra[1]
        s = (across[m * KA : (m + 1) * KA] + along) * root_ref[...]
        s_ref[pl.ds(pl.multiple_of((to + m) * KA, 8), KA), :] = s
        square_ref[pl.ds(to + m, 1), :] = jnp.sum(s * s, axis=0, keepdims=True)


def smooth_top_kernel(t_ref, r0, r1, rc, ro, root_ref, band_ref, s_ref, square_ref, side_ref, south_ref):
    north, south, west, east = halos(r0, r1, rc, ro)
    low = iota((KA, N), 1) < 64
    side_ref[...] = jnp.where(low, pltpu.roll(west, 64, 1), east).astype(BF16)
    south_ref[...] = south
    side = jnp.where(low, west, pltpu.roll(east, 64, 1)).astype(BF16)

    def rows(i, _):
        beyond = jnp.where(i == 0, north, 0.0)
        smooth_rows(t_ref, side, root_ref, band_ref, s_ref, square_ref, 32 * i, 32, 32 * i, (0, beyond))
        return 0

    lax.fori_loop(0, 2, rows, 0)
    if TOP > 64:
        smooth_rows(t_ref, side_ref[...], root_ref, band_ref, s_ref, square_ref, 64, TOP - 64, 64)


def smooth_bottom_kernel(t_ref, side_ref, south_ref, root_ref, band_ref, s_ref, square_ref):
    count = (N - TOP) // 2

    def rows(i, _):
        beyond = jnp.where(i == 1, south_ref[...], 0.0)
        row = TOP + count * i
        smooth_rows(t_ref, side_ref[...], root_ref, band_ref, s_ref, square_ref, row, count, count * i, (count - 1, beyond))
        return 0

    lax.fori_loop(0, 2, rows, 0)


def final_kernel(p0, p1, p2, p3, s0_ref, s1_ref, square0, square1, lab_ref, own_ref, root_ref, out_ref, e_ref):
    own = own_ref[...]
    lefts, rights = [], []
    for p in (p0, p1, p2, p3):
        pay = p[...]
        gl = pay[LEV + 2 : LEV + 3].astype(F32) * 64.0 + pay[LEV + 3 : LEV + 4].astype(F32)
        lefts.append(pay)
        rights.append(jnp.where(own == gl, 1.0, 0.0).astype(BF16))
    total = dot(jnp.concatenate(lefts, axis=1), jnp.concatenate(rights, axis=1), NT)
    count = 256.0 * total[LEV : LEV + 1] + 32.0 * total[LEV + 1 : LEV + 2]
    profile = root_ref[...] * (total * (8.0 / jnp.maximum(count, 1.0)))
    hi = profile.astype(BF16).astype(F32)
    lo = (profile - hi).astype(BF16).astype(F32)
    profile = hi + lo
    energy = jnp.sum(profile * profile, axis=0, keepdims=True)
    energy_hi = energy.astype(BF16).astype(F32)
    row = iota((KA, N), 0)
    hi = jnp.where(row == LEV, energy_hi, hi).astype(BF16)
    lo = jnp.where(row == LEV, energy - energy_hi, lo).astype(BF16)
    left = jnp.concatenate([hi, lo], axis=1)
    ids = iota((N, N), 0).astype(F32).astype(BF16)

    def patch_row(q, s_ref, top):
        row = lab_ref[pl.ds(4 * q, 1), :].astype(F32).astype(BF16)
        mark = jnp.where(row == ids, BF16(1.0), BF16(0.0))
        placed = dot(left, jnp.concatenate([mark, mark], axis=0), NN)
        e_ref[pl.ds(4 * q, 4), :] = placed[LEV : LEV + 1] + jnp.zeros((4, N), F32)
        for m in range(4):
            r = 4 * q + m
            cross = s_ref[pl.ds((r - top) * KA, KA), :] * placed
            out_ref[pl.ds(r, 1), :] = jnp.sum(cross, axis=0, keepdims=True)

    for q in range(N // 4):
        if 4 * q < TOP:
            patch_row(q, s0_ref, 0)
        else:
            patch_row(q, s1_ref, TOP)
    e = e_ref[...]
    square = jnp.concatenate([square0[...], square1[...]], axis=0)
    out_ref[...] = jnp.sqrt(jnp.maximum(square - 2.0 * out_ref[...] + e, 0.0) / e)


def vertical(turn):
    pairs = []
    for i in range(8):
        for j in range(16):
            if (j % 4 < 2) == (turn == 0):
                other = 16 * i + (j ^ 1) if i in (0, 7) else 16 * (i + 1 if i % 2 else i - 1) + j
            else:
                other = 16 * (i ^ 1) + j
            pairs.append((16 * i + j, other))
    return pairs


def params(mib):
    return pltpu.CompilerParams(vmem_limit_bytes=mib * 1024 * 1024)


def cost(flops, moved):
    return pl.CostEstimate(flops=flops, bytes_accessed=moved, transcendentals=0)


def shards(humidity, wind_u, wind_v, weights, labels, global_labels):
    vmem = pl.BlockSpec(memory_space=pltpu.VMEM)
    anywhere = pl.BlockSpec(memory_space=pl.ANY)
    edge = pltpu.VMEM((KA, N), BF16)
    wide = pltpu.VMEM((KA, N), F32)
    gl = global_labels.reshape(1, N)
    w = weights.reshape(1, LEV)
    t, s0, s1, c0, c1 = pl.pallas_call(
        transport_kernel,
        out_shape=(pltpu.VMEM(((N + 2) * KP, N), F32), edge, edge, edge, edge),
        in_specs=[anywhere] * 3,
        out_specs=[vmem] * 5,
        scratch_shapes=[pltpu.VMEM((LEV, N, N), BF16)] * 3
        + [pltpu.VMEM((3, N, N), BF16), pltpu.VMEM((N, N), BF16), pltpu.VMEM((2, KA, 3 * N), BF16)]
        + [pltpu.SemaphoreType.DMA((len(CHUNKS), 3))],
        compiler_params=params(18),
        cost_estimate=cost(30_000_000, 23_000_000),
        name="transport",
    )(*(pltpu.with_memory_space_constraint(x, pltpu.HBM) for x in (humidity, wind_u, wind_v)))
    r0 = lax.ppermute(s0, ("lat", "lon"), vertical(0))
    r1 = lax.ppermute(s1, ("lat", "lon"), vertical(1))
    ro = lax.ppermute(c1, "lon", [(j, (j + 1) % 16 if j % 2 else (j - 1) % 16) for j in range(16)])
    rc = lax.ppermute(c0, "lon", [(j, j ^ 1) for j in range(16)])
    t0, root, own, band = pl.pallas_call(
        sums_kernel,
        out_shape=(wide, wide, pltpu.VMEM((N, N), F32), pltpu.VMEM((2 * N, N), BF16)),
        in_specs=[vmem] * 4,
        out_specs=[vmem] * 4,
        scratch_shapes=[pltpu.VMEM((N, N), jnp.int32)] * 2,
        compiler_params=params(8),
        cost_estimate=cost(600_000_000, 9_500_000),
        name="sums",
    )(t, labels, gl, w)
    pay = pl.pallas_call(
        pack_kernel,
        out_shape=edge,
        in_specs=[vmem] * 7,
        out_specs=vmem,
        compiler_params=params(8),
        cost_estimate=cost(20_000_000, 300_000),
        name="pack",
    )(t0, r0, r1, ro, rc, labels, gl)
    p2 = lax.ppermute(pay, "lat", [(i, (i + 4) % 8) for i in range(8)])
    p1 = lax.ppermute(pay, "lon", [(j, j ^ 1) for j in range(16)])
    p3 = lax.ppermute(p2, "lon", [(j, j ^ 1) for j in range(16)])
    top0, square0, side, south = pl.pallas_call(
        smooth_top_kernel,
        out_shape=(pltpu.VMEM((TOP * KA, N), F32), pltpu.VMEM((TOP, N), F32), edge, wide),
        in_specs=[vmem] * 7,
        out_specs=[vmem] * 4,
        compiler_params=params(12),
        cost_estimate=cost(600_000_000, 9_500_000),
        name="smooth_top",
    )(t, r0, r1, rc, ro, root, band)
    bottom, square1 = pl.pallas_call(
        smooth_bottom_kernel,
        out_shape=(pltpu.VMEM(((N - TOP) * KA, N), F32), pltpu.VMEM((N - TOP, N), F32)),
        in_specs=[vmem] * 5,
        out_specs=[vmem] * 2,
        compiler_params=params(12),
        cost_estimate=cost(600_000_000, 9_500_000),
        name="smooth_bottom",
    )(t, side, south, root, band)
    return pl.pallas_call(
        final_kernel,
        out_shape=jax.ShapeDtypeStruct((N, N), F32),
        in_specs=[vmem] * 11,
        out_specs=vmem,
        scratch_shapes=[pltpu.VMEM((N, N), F32)],
        compiler_params=params(8),
        cost_estimate=cost(300_000_000, 9_500_000),
        name="final",
    )(pay, p1, p2, p3, top0, bottom, square0, square1, labels, own, root)


def solution(mesh):
    return jax.shard_map(
        shards,
        mesh=mesh,
        in_specs=(
            P(None, "lat", "lon"),
            P(None, "lat", "lon"),
            P(None, "lat", "lon"),
            P(),
            P("lat", "lon"),
            P("lat", "lon", None),
        ),
        out_specs=P("lat", "lon"),
        check_vma=False,
    )
```

```python
import jax
import jax.numpy as jnp
from jax import lax
from jax.experimental import pallas as pl
from jax.experimental.pallas import tpu as pltpu
from jax.sharding import PartitionSpec as P

F32 = jnp.float32
BF16 = jnp.bfloat16
LEV = 137
KA = 144
TOP = 88
KP = 152
N = 128
CHUNKS = ((0, 8), (8, 16), (24, 24), (48, 24), (72, 24), (96, 24), (120, 8), (128, 9))
NT = (((1,), (1,)), ((), ()))
NN = (((1,), (0,)), ((), ()))


def iota(shape, dim):
    return lax.broadcasted_iota(jnp.int32, shape, dim)


def dot(a, b, dims):
    return lax.dot_general(a, b, dims, preferred_element_type=F32)


def column(row, rows):
    shape = (rows, row.shape[1])
    return jnp.sum(jnp.where(iota(shape, 0) == iota(shape, 1), row, 0.0), axis=1, keepdims=True)


def ends():
    shape = (16, N)
    first = (iota(shape, 0) == 0) & (iota(shape, 1) == 0)
    last = (iota(shape, 0) == 1) & (iota(shape, 1) == N - 1)
    return jnp.where(first | last, 1.0, 0.0).astype(BF16)


def north_first():
    i, j = lax.axis_index("lat"), lax.axis_index("lon")
    return (lax.rem(i, 2) == 0) == (lax.rem(j, 4) < 2)


def halos(r0, r1, rc, ro):
    i, j = lax.axis_index("lat"), lax.axis_index("lon")
    first, j_even = north_first(), lax.rem(j, 2) == 0
    r0, r1, rc, ro = (r[...].astype(F32) for r in (r0, r1, rc, ro))
    north = jnp.where(i == 0, 0.0, jnp.where(first, r0, r1))
    south = jnp.where(i == 7, 0.0, jnp.where(first, r1, r0))
    west = jnp.where(j_even, ro, rc)
    east = jnp.where(j_even, rc, ro)
    return north, south, west, east


def transport_kernel(h_hbm, u_hbm, v_hbm, t_ref, s0_ref, s1_ref, c0_ref, c1_ref, hb, ub, vb, cols, near, picks, sems):
    copies = []
    for c, (a, n) in enumerate(CHUNKS):
        row = []
        for m, (src, dst) in enumerate(((h_hbm, hb), (u_hbm, ub), (v_hbm, vb))):
            copy = pltpu.make_async_copy(src.at[pl.ds(a, n)], dst.at[pl.ds(a, n)], sems.at[c, m])
            copy.start()
            row.append(copy)
        copies.append(row)
    zeros = jnp.zeros((N, N), F32)
    for k in range(LEV, KA):
        t_ref[pl.ds(KP + k, N, stride=KP), :] = zeros
    blank = jnp.zeros((KA, N), F32)
    t_ref[pl.ds(0, KA), :] = blank
    t_ref[pl.ds((N + 1) * KP, KA), :] = blank
    cols[...] = jnp.zeros((3, N, N), BF16)
    lane = iota((N, N), 1)
    first, j_even = north_first(), lax.rem(lax.axis_index("lon"), 2) == 0
    k, at = iota((KA, 3 * N), 0), iota((KA, 3 * N), 1)
    left_at = 2 * k
    right_at = jnp.where(lax.rem(k, 64) == 0, 2 * k + N - 1, 2 * k - 1)
    picks[0] = jnp.where(at == jnp.where(j_even, right_at, left_at), 1.0, 0.0).astype(BF16)
    picks[1] = jnp.where(at == jnp.where(j_even, left_at, right_at), 1.0, 0.0).astype(BF16)

    def level(k):
        parts = []
        for b in range(0, N, 32):
            rows = pl.ds(b, 32)
            u, v = ub[k, rows, :], vb[k, rows, :]
            x = (u * u + v * v).astype(F32) + 1.0
            t = hb[k, rows, :].astype(F32) * (x * lax.rsqrt(x))
            t_ref[pl.ds((1 + b) * KP + k, 32, stride=KP), :] = t
            parts.append(t.astype(BF16))
        return jnp.concatenate(parts, axis=0)

    def group(k, size):
        ends = level(k)
        for q in range(1, size):
            moved = pltpu.roll(level(k + q), 2 * q, 1)
            ends = jnp.where((lane == 2 * q) | (lane == 2 * q - 1), moved, ends)
        near[...] = ends

    def merge(k, size):
        shift = 2 * lax.rem(k, 64)
        mine = lax.rem(lane - shift + N + 1, N) < 2 * size
        block = lax.div(k, 64)
        cols[block] = jnp.where(mine, pltpu.roll(near[...], shift, 1), cols[block])

    for (a, n), row in zip(CHUNKS, copies):
        for copy in row:
            copy.wait()

        def groups(g, _, a=a):
            merge(a + 8 * g - 8, 8)
            group(a + 8 * g, 8)
            return 0

        if a == 0:
            group(0, 8)
        lax.fori_loop(1 if a == 0 else 0, n // 8, groups, 0)
        if n % 8:
            end = a + n - n % 8
            merge(end - 8, 8)
            group(end, n % 8)
            merge(end, n % 8)

    def row_at(top):
        start = pl.multiple_of(jnp.where(top, KP, N * KP), 8)
        return t_ref[pl.ds(start, KA), :].astype(BF16)

    packed = jnp.concatenate([cols[0], cols[1], cols[2]], axis=1)
    s0_ref[...] = row_at(first)
    s1_ref[...] = row_at(jnp.logical_not(first))
    c0_ref[...] = dot(picks[0], packed, NT).astype(BF16)
    c1_ref[...] = dot(picks[1], packed, NT).astype(BF16)


def sums_kernel(t_ref, lab_ref, gl_ref, w_ref, t0_ref, root_ref, own_ref, band_ref, marks_ref, west_ref, east_ref):
    root_ref[...] = jnp.sqrt(column(w_ref[...], KA)) * 0.125 + jnp.zeros((KA, N), F32)
    own_ref[...] = column(gl_ref[...].astype(F32), N) + jnp.zeros((N, N), F32)
    a, c = iota((2 * N, N), 0), iota((2 * N, N), 1)
    band = jnp.where(a == c, 4.0, jnp.where(jnp.abs(a - c) == 1, 1.0, 0.0))
    edge = jnp.where(c == jnp.where(a < N + 64, 0, N - 1), 1.0, 0.0)
    band_ref[...] = jnp.where(a < N, band, edge).astype(BF16)
    lab = lab_ref[...]
    lane = iota((N, N), 1)
    west_ref[...] = jnp.where(lane == 0, -1, pltpu.roll(lab, 1, 1))
    east_ref[...] = jnp.where(lane == N - 1, -1, pltpu.roll(lab, N - 1, 1))
    ids = iota((N, N), 0).astype(F32).astype(BF16)
    t0_ref[...] = jnp.zeros((KA, N), F32)
    last = iota((8, N), 0) + (LEV - LEV % 8)

    def patch_row(q):
        base = pl.multiple_of((1 + 4 * q) * KP, 8)
        x = [t_ref[pl.ds(base + m * KP, KA), :] for m in range(-1, 5)]
        whole = x[1] + x[2] + x[3] + x[4]
        step = (x[0] - x[4]) + (x[5] - x[1])
        step = jnp.concatenate([step[: LEV - LEV % 8], jnp.where(last == LEV, 32.0, step[LEV - LEV % 8 :])], axis=0)
        left = jnp.concatenate([whole.astype(BF16), step.astype(BF16)], axis=1)

        def marks(ref):
            row = ref[pl.ds(4 * q, 1), :].astype(F32).astype(BF16)
            return jnp.where(row == ids, BF16(0.125), BF16(0.0))

        here = marks(lab_ref)
        spread = here * BF16(6.0) + (marks(west_ref) + marks(east_ref))
        return left, jnp.concatenate([spread, here], axis=1)

    def patch_rows(i, _):
        pairs = [patch_row(16 * i + m) for m in range(16)]
        left, right = (jnp.concatenate(p, axis=1) for p in zip(*pairs))
        t0_ref[...] += dot(left, right, NT)
        return 0

    lax.fori_loop(0, N // 64, patch_rows, 0)
    total = t0_ref[LEV - LEV % 8 :, :]
    count = total[LEV % 8 : LEV % 8 + 1] * (1.0 / 32.0)
    count_hi = jnp.floor(count * 0.125)
    gl = gl_ref[...].astype(F32)
    gl_hi = jnp.floor(gl * (1.0 / 64.0))
    for m, extra in enumerate((count_hi, count - 8.0 * count_hi, gl_hi, gl - 64.0 * gl_hi)):
        total = jnp.where(last == LEV + m, extra, total)
    t0_ref[LEV - LEV % 8 :, :] = total

    sides = dot(ends(), lab.astype(F32).astype(BF16), NT)
    rows = iota((N, N), 0).astype(F32)

    def edge_marks(row, there):
        return jnp.where((row == rows) & there, 0.125, 0.0)

    i, j = lax.axis_index("lat"), lax.axis_index("lon")
    up, j_even = north_first(), lax.rem(j, 2) == 0
    north = edge_marks(lab[0:1].astype(F32), i > 0)
    south = edge_marks(lab[N - 1 : N].astype(F32), i < 7)
    west, east = edge_marks(sides[0:1], True), edge_marks(sides[1:2], True)
    marks_ref[...] = jnp.concatenate(
        [jnp.where(up, north, south), jnp.where(up, south, north), jnp.where(j_even, west, east), jnp.where(j_even, east, west)],
        axis=1,
    ).astype(BF16)


def pack_kernel(t0_ref, r0, r1, ro, rc, marks_ref, pay_ref):
    left = jnp.concatenate([r0[...], r1[...], ro[...], rc[...]], axis=1)
    pay_ref[...] = (t0_ref[...] + dot(left, marks_ref[...], NT)).astype(BF16)


def smooth_rows(t_ref, side, root_ref, band_ref, s_ref, square_ref, row, count, to, extra=None):
    lane = lax.rem(iota((1, N), 1), 64)

    def at(r):
        return pl.ds(pl.multiple_of(r * KP, 8), KA)

    lefts = []
    for m in range(count):
        mine = jnp.where(lane == lax.rem(row + m, 64), 1.0, 0.0).astype(BF16)
        lefts.append(jnp.concatenate([t_ref[at(row + m + 1), :].astype(BF16), side * mine], axis=1))
    across = dot(jnp.concatenate(lefts, axis=0), band_ref[...], NN)
    for m in range(count):
        along = t_ref[at(row + m), :] + t_ref[at(row + m + 2), :]
        if extra is not None and m == extra[0]:
            along = along + extra[1]
        s = (across[m * KA : (m + 1) * KA] + along) * root_ref[...]
        s_ref[pl.ds(pl.multiple_of((to + m) * KA, 8), KA), :] = s
        square_ref[pl.ds(to + m, 1), :] = jnp.sum(s * s, axis=0, keepdims=True)


def smooth_top_kernel(t_ref, r0, r1, rc, ro, root_ref, band_ref, s_ref, square_ref, side_ref, south_ref):
    north, south, west, east = halos(r0, r1, rc, ro)
    low = iota((KA, N), 1) < 64
    side_ref[...] = jnp.where(low, pltpu.roll(west, 64, 1), east).astype(BF16)
    south_ref[...] = south
    side = jnp.where(low, west, pltpu.roll(east, 64, 1)).astype(BF16)

    def rows(i, _):
        beyond = jnp.where(i == 0, north, 0.0)
        smooth_rows(t_ref, side, root_ref, band_ref, s_ref, square_ref, 32 * i, 32, 32 * i, (0, beyond))
        return 0

    lax.fori_loop(0, 2, rows, 0)
    if TOP > 64:
        smooth_rows(t_ref, side_ref[...], root_ref, band_ref, s_ref, square_ref, 64, TOP - 64, 64)


def smooth_bottom_kernel(t_ref, side_ref, south_ref, root_ref, band_ref, s_ref, square_ref):
    count = (N - TOP) // 2

    def rows(i, _):
        beyond = jnp.where(i == 1, south_ref[...], 0.0)
        row = TOP + count * i
        smooth_rows(t_ref, side_ref[...], root_ref, band_ref, s_ref, square_ref, row, count, count * i, (count - 1, beyond))
        return 0

    lax.fori_loop(0, 2, rows, 0)


def final_kernel(p0, p1, p2, p3, s0_ref, s1_ref, square0, square1, lab_ref, own_ref, root_ref, out_ref, e_ref):
    own = own_ref[...]
    lefts, rights = [], []
    for p in (p0, p1, p2, p3):
        pay = p[...]
        gl = pay[LEV + 2 : LEV + 3].astype(F32) * 64.0 + pay[LEV + 3 : LEV + 4].astype(F32)
        lefts.append(pay)
        rights.append(jnp.where(own == gl, 1.0, 0.0).astype(BF16))
    total = dot(jnp.concatenate(lefts, axis=1), jnp.concatenate(rights, axis=1), NT)
    count = 256.0 * total[LEV : LEV + 1] + 32.0 * total[LEV + 1 : LEV + 2]
    profile = root_ref[...] * (total * (8.0 / jnp.maximum(count, 1.0)))
    hi = profile.astype(BF16).astype(F32)
    lo = (profile - hi).astype(BF16).astype(F32)
    profile = hi + lo
    energy = jnp.sum(profile * profile, axis=0, keepdims=True)
    energy_hi = energy.astype(BF16).astype(F32)
    row = iota((KA, N), 0)
    hi = jnp.where(row == LEV, energy_hi, hi).astype(BF16)
    lo = jnp.where(row == LEV, energy - energy_hi, lo).astype(BF16)
    left = jnp.concatenate([hi, lo], axis=1)
    ids = iota((N, N), 0).astype(F32).astype(BF16)

    def patch_row(q, s_ref, top):
        row = lab_ref[pl.ds(4 * q, 1), :].astype(F32).astype(BF16)
        mark = jnp.where(row == ids, BF16(1.0), BF16(0.0))
        placed = dot(left, jnp.concatenate([mark, mark], axis=0), NN)
        e_ref[pl.ds(4 * q, 4), :] = placed[LEV : LEV + 1] + jnp.zeros((4, N), F32)
        for m in range(4):
            r = 4 * q + m
            cross = s_ref[pl.ds((r - top) * KA, KA), :] * placed
            out_ref[pl.ds(r, 1), :] = jnp.sum(cross, axis=0, keepdims=True)

    for q in range(N // 4):
        if 4 * q < TOP:
            patch_row(q, s0_ref, 0)
        else:
            patch_row(q, s1_ref, TOP)
    e = e_ref[...]
    square = jnp.concatenate([square0[...], square1[...]], axis=0)
    out_ref[...] = jnp.sqrt(jnp.maximum(square - 2.0 * out_ref[...] + e, 0.0) / e)


def vertical(turn):
    pairs = []
    for i in range(8):
        for j in range(16):
            if (j % 4 < 2) == (turn == 0):
                other = 16 * i + (j ^ 1) if i in (0, 7) else 16 * (i + 1 if i % 2 else i - 1) + j
            else:
                other = 16 * (i ^ 1) + j
            pairs.append((16 * i + j, other))
    return pairs


def params(mib):
    return pltpu.CompilerParams(vmem_limit_bytes=mib * 1024 * 1024)


def cost(flops, moved):
    return pl.CostEstimate(flops=flops, bytes_accessed=moved, transcendentals=0)


def shards(humidity, wind_u, wind_v, weights, labels, global_labels):
    vmem = pl.BlockSpec(memory_space=pltpu.VMEM)
    anywhere = pl.BlockSpec(memory_space=pl.ANY)
    edge = pltpu.VMEM((KA, N), BF16)
    wide = pltpu.VMEM((KA, N), F32)
    gl = global_labels.reshape(1, N)
    w = weights.reshape(1, LEV)
    t, s0, s1, c0, c1 = pl.pallas_call(
        transport_kernel,
        out_shape=(pltpu.VMEM(((N + 2) * KP, N), F32), edge, edge, edge, edge),
        in_specs=[anywhere] * 3,
        out_specs=[vmem] * 5,
        scratch_shapes=[pltpu.VMEM((LEV, N, N), BF16)] * 3
        + [pltpu.VMEM((3, N, N), BF16), pltpu.VMEM((N, N), BF16), pltpu.VMEM((2, KA, 3 * N), BF16)]
        + [pltpu.SemaphoreType.DMA((len(CHUNKS), 3))],
        compiler_params=params(18),
        cost_estimate=cost(30_000_000, 23_000_000),
        name="transport",
    )(*(pltpu.with_memory_space_constraint(x, pltpu.HBM) for x in (humidity, wind_u, wind_v)))
    r0 = lax.ppermute(s0, ("lat", "lon"), vertical(0))
    r1 = lax.ppermute(s1, ("lat", "lon"), vertical(1))
    ro = lax.ppermute(c1, "lon", [(j, (j + 1) % 16 if j % 2 else (j - 1) % 16) for j in range(16)])
    rc = lax.ppermute(c0, "lon", [(j, j ^ 1) for j in range(16)])
    t0, root, own, band, marks = pl.pallas_call(
        sums_kernel,
        out_shape=(wide, wide, pltpu.VMEM((N, N), F32), pltpu.VMEM((2 * N, N), BF16), pltpu.VMEM((N, 4 * N), BF16)),
        in_specs=[vmem] * 4,
        out_specs=[vmem] * 5,
        scratch_shapes=[pltpu.VMEM((N, N), jnp.int32)] * 2,
        compiler_params=params(8),
        cost_estimate=cost(600_000_000, 9_500_000),
        name="sums",
    )(t, labels, gl, w)
    pay = pl.pallas_call(
        pack_kernel,
        out_shape=edge,
        in_specs=[vmem] * 6,
        out_specs=vmem,
        compiler_params=params(8),
        cost_estimate=cost(20_000_000, 300_000),
        name="pack",
    )(t0, r0, r1, ro, rc, marks)
    p2 = lax.ppermute(pay, "lat", [(i, (i + 4) % 8) for i in range(8)])
    p1 = lax.ppermute(pay, "lon", [(j, j ^ 1) for j in range(16)])
    p3 = lax.ppermute(p2, "lon", [(j, j ^ 1) for j in range(16)])
    top0, square0, side, south = pl.pallas_call(
        smooth_top_kernel,
        out_shape=(pltpu.VMEM((TOP * KA, N), F32), pltpu.VMEM((TOP, N), F32), edge, wide),
        in_specs=[vmem] * 7,
        out_specs=[vmem] * 4,
        compiler_params=params(12),
        cost_estimate=cost(600_000_000, 9_500_000),
        name="smooth_top",
    )(t, r0, r1, rc, ro, root, band)
    bottom, square1 = pl.pallas_call(
        smooth_bottom_kernel,
        out_shape=(pltpu.VMEM(((N - TOP) * KA, N), F32), pltpu.VMEM((N - TOP, N), F32)),
        in_specs=[vmem] * 5,
        out_specs=[vmem] * 2,
        compiler_params=params(12),
        cost_estimate=cost(600_000_000, 9_500_000),
        name="smooth_bottom",
    )(t, side, south, root, band)
    return pl.pallas_call(
        final_kernel,
        out_shape=jax.ShapeDtypeStruct((N, N), F32),
        in_specs=[vmem] * 11,
        out_specs=vmem,
        scratch_shapes=[pltpu.VMEM((N, N), F32)],
        compiler_params=params(8),
        cost_estimate=cost(300_000_000, 9_500_000),
        name="final",
    )(pay, p1, p2, p3, top0, bottom, square0, square1, labels, own, root)


def solution(mesh):
    return jax.shard_map(
        shards,
        mesh=mesh,
        in_specs=(
            P(None, "lat", "lon"),
            P(None, "lat", "lon"),
            P(None, "lat", "lon"),
            P(),
            P("lat", "lon"),
            P("lat", "lon", None),
        ),
        out_specs=P("lat", "lon"),
        check_vma=False,
    )
```

```python
import jax
import jax.numpy as jnp
from jax import lax
from jax.experimental import pallas as pl
from jax.experimental.pallas import tpu as pltpu
from jax.sharding import PartitionSpec as P

F32 = jnp.float32
BF16 = jnp.bfloat16
LEV = 137
KA = 144
TOP = 88
KP = 152
N = 128
CHUNKS = ((0, 8), (8, 16), (24, 24), (48, 24), (72, 24), (96, 24), (120, 8), (128, 9))
NT = (((1,), (1,)), ((), ()))
NN = (((1,), (0,)), ((), ()))


def iota(shape, dim):
    return lax.broadcasted_iota(jnp.int32, shape, dim)


def dot(a, b, dims):
    return lax.dot_general(a, b, dims, preferred_element_type=F32)


def column(row, rows):
    shape = (rows, row.shape[1])
    return jnp.sum(jnp.where(iota(shape, 0) == iota(shape, 1), row, 0.0), axis=1, keepdims=True)


def ends():
    shape = (16, N)
    first = (iota(shape, 0) == 0) & (iota(shape, 1) == 0)
    last = (iota(shape, 0) == 1) & (iota(shape, 1) == N - 1)
    return jnp.where(first | last, 1.0, 0.0).astype(BF16)


def north_first():
    i, j = lax.axis_index("lat"), lax.axis_index("lon")
    return (lax.rem(i, 2) == 0) == (lax.rem(j, 4) < 2)


def halos(r0, r1, rc, ro):
    i, j = lax.axis_index("lat"), lax.axis_index("lon")
    first, j_even = north_first(), lax.rem(j, 2) == 0
    r0, r1, rc, ro = (r[...].astype(F32) for r in (r0, r1, rc, ro))
    north = jnp.where(i == 0, 0.0, jnp.where(first, r0, r1))
    south = jnp.where(i == 7, 0.0, jnp.where(first, r1, r0))
    west = jnp.where(j_even, ro, rc)
    east = jnp.where(j_even, rc, ro)
    return north, south, west, east


def transport_kernel(h_hbm, u_hbm, v_hbm, t_ref, s0_ref, s1_ref, c0_ref, c1_ref, band_ref, hb, ub, vb, cols, near, picks, sems):
    copies = []
    for c, (a, n) in enumerate(CHUNKS):
        row = []
        for m, (src, dst) in enumerate(((h_hbm, hb), (u_hbm, ub), (v_hbm, vb))):
            copy = pltpu.make_async_copy(src.at[pl.ds(a, n)], dst.at[pl.ds(a, n)], sems.at[c, m])
            copy.start()
            row.append(copy)
        copies.append(row)
    zeros = jnp.zeros((N, N), F32)
    for k in range(LEV, KA):
        t_ref[pl.ds(KP + k, N, stride=KP), :] = zeros
    blank = jnp.zeros((KA, N), F32)
    t_ref[pl.ds(0, KA), :] = blank
    t_ref[pl.ds((N + 1) * KP, KA), :] = blank
    cols[...] = jnp.zeros((3, N, N), BF16)
    lane = iota((N, N), 1)
    first, j_even = north_first(), lax.rem(lax.axis_index("lon"), 2) == 0
    k, at = iota((KA, 3 * N), 0), iota((KA, 3 * N), 1)
    left_at = 2 * k
    right_at = jnp.where(lax.rem(k, 64) == 0, 2 * k + N - 1, 2 * k - 1)
    picks[0] = jnp.where(at == jnp.where(j_even, right_at, left_at), 1.0, 0.0).astype(BF16)
    picks[1] = jnp.where(at == jnp.where(j_even, left_at, right_at), 1.0, 0.0).astype(BF16)

    a, c = iota((3 * N, 2 * N), 0), iota((3 * N, 2 * N), 1)
    a_in, a_of, c_in, c_of = lax.rem(a, N), lax.div(a, N), lax.rem(c, N), lax.div(c, N)
    band = jnp.where(a_in == c_in, 4.0, jnp.where(jnp.abs(a_in - c_in) == 1, 1.0, 0.0))
    edge = jnp.where(c_in == jnp.where(a_in < 64, 0, N - 1), 1.0, 0.0)
    edge = jnp.where(lax.rem(a, 2) == c_of, edge, 0.0)
    band_ref[...] = jnp.where(a_of == 2, edge, jnp.where(a_of == c_of, band, 0.0)).astype(BF16)

    def level(k):
        parts = []
        for b in range(0, N, 32):
            rows = pl.ds(b, 32)
            u, v = ub[k, rows, :], vb[k, rows, :]
            x = (u * u + v * v).astype(F32) + 1.0
            t = hb[k, rows, :].astype(F32) * (x * lax.rsqrt(x))
            t_ref[pl.ds((1 + b) * KP + k, 32, stride=KP), :] = t
            parts.append(t.astype(BF16))
        return jnp.concatenate(parts, axis=0)

    def group(k, size):
        ends = level(k)
        for q in range(1, size):
            moved = pltpu.roll(level(k + q), 2 * q, 1)
            ends = jnp.where((lane == 2 * q) | (lane == 2 * q - 1), moved, ends)
        near[...] = ends

    def merge(k, size):
        shift = 2 * lax.rem(k, 64)
        mine = lax.rem(lane - shift + N + 1, N) < 2 * size
        block = lax.div(k, 64)
        cols[block] = jnp.where(mine, pltpu.roll(near[...], shift, 1), cols[block])

    for (a, n), row in zip(CHUNKS, copies):
        for copy in row:
            copy.wait()

        def groups(g, _, a=a):
            merge(a + 8 * g - 8, 8)
            group(a + 8 * g, 8)
            return 0

        if a == 0:
            group(0, 8)
        lax.fori_loop(1 if a == 0 else 0, n // 8, groups, 0)
        if n % 8:
            end = a + n - n % 8
            merge(end - 8, 8)
            group(end, n % 8)
            merge(end, n % 8)

    def row_at(top):
        start = pl.multiple_of(jnp.where(top, KP, N * KP), 8)
        return t_ref[pl.ds(start, KA), :].astype(BF16)

    packed = jnp.concatenate([cols[0], cols[1], cols[2]], axis=1)
    s0_ref[...] = row_at(first)
    s1_ref[...] = row_at(jnp.logical_not(first))
    c0_ref[...] = dot(picks[0], packed, NT).astype(BF16)
    c1_ref[...] = dot(picks[1], packed, NT).astype(BF16)


def sums_kernel(t_ref, lab_ref, gl_ref, w_ref, t0_ref, root_ref, own_ref, marks_ref, west_ref, east_ref):
    root_ref[...] = jnp.sqrt(column(w_ref[...], KA)) * 0.125 + jnp.zeros((KA, N), F32)
    own_ref[...] = column(gl_ref[...].astype(F32), N) + jnp.zeros((N, N), F32)
    lab = lab_ref[...]
    lane = iota((N, N), 1)
    west_ref[...] = jnp.where(lane == 0, -1, pltpu.roll(lab, 1, 1))
    east_ref[...] = jnp.where(lane == N - 1, -1, pltpu.roll(lab, N - 1, 1))
    ids = iota((N, N), 0).astype(F32).astype(BF16)
    t0_ref[...] = jnp.zeros((KA, N), F32)
    last = iota((8, N), 0) + (LEV - LEV % 8)

    def patch_row(q):
        base = pl.multiple_of((1 + 4 * q) * KP, 8)
        x = [t_ref[pl.ds(base + m * KP, KA), :] for m in range(-1, 5)]
        whole = x[1] + x[2] + x[3] + x[4]
        step = (x[0] - x[4]) + (x[5] - x[1])
        step = jnp.concatenate([step[: LEV - LEV % 8], jnp.where(last == LEV, 32.0, step[LEV - LEV % 8 :])], axis=0)
        left = jnp.concatenate([whole.astype(BF16), step.astype(BF16)], axis=1)

        def marks(ref):
            row = ref[pl.ds(4 * q, 1), :].astype(F32).astype(BF16)
            return jnp.where(row == ids, BF16(0.125), BF16(0.0))

        here = marks(lab_ref)
        spread = here * BF16(6.0) + (marks(west_ref) + marks(east_ref))
        return left, jnp.concatenate([spread, here], axis=1)

    def patch_rows(i, _):
        pairs = [patch_row(16 * i + m) for m in range(16)]
        left, right = (jnp.concatenate(p, axis=1) for p in zip(*pairs))
        t0_ref[...] += dot(left, right, NT)
        return 0

    lax.fori_loop(0, N // 64, patch_rows, 0)
    total = t0_ref[LEV - LEV % 8 :, :]
    count = total[LEV % 8 : LEV % 8 + 1] * (1.0 / 32.0)
    count_hi = jnp.floor(count * 0.125)
    gl = gl_ref[...].astype(F32)
    gl_hi = jnp.floor(gl * (1.0 / 64.0))
    for m, extra in enumerate((count_hi, count - 8.0 * count_hi, gl_hi, gl - 64.0 * gl_hi)):
        total = jnp.where(last == LEV + m, extra, total)
    t0_ref[LEV - LEV % 8 :, :] = total

    sides = dot(ends(), lab.astype(F32).astype(BF16), NT)
    rows = iota((N, N), 0).astype(F32)

    def edge_marks(row, there):
        return jnp.where((row == rows) & there, 0.125, 0.0)

    i, j = lax.axis_index("lat"), lax.axis_index("lon")
    up, j_even = north_first(), lax.rem(j, 2) == 0
    north = edge_marks(lab[0:1].astype(F32), i > 0)
    south = edge_marks(lab[N - 1 : N].astype(F32), i < 7)
    west, east = edge_marks(sides[0:1], True), edge_marks(sides[1:2], True)
    marks_ref[...] = jnp.concatenate(
        [jnp.where(up, north, south), jnp.where(up, south, north), jnp.where(j_even, west, east), jnp.where(j_even, east, west)],
        axis=1,
    ).astype(BF16)


def pack_kernel(t0_ref, r0, r1, ro, rc, marks_ref, pay_ref):
    left = jnp.concatenate([r0[...], r1[...], ro[...], rc[...]], axis=1)
    pay_ref[...] = (t0_ref[...] + dot(left, marks_ref[...], NT)).astype(BF16)


def smooth_rows(t_ref, side, root_ref, band_ref, s_ref, square_ref, row, count, to, extra=None):
    pair = lax.div(lax.rem(iota((1, N), 1), 64), 2)

    def at(r):
        return pl.ds(pl.multiple_of(r * KP, 8), KA)

    lefts = []
    for m in range(0, count, 2):
        mine = jnp.where(pair == lax.div(lax.rem(row + m, 64), 2), 1.0, 0.0).astype(BF16)
        two = [t_ref[at(row + m + n), :].astype(BF16) for n in (1, 2)]
        lefts.append(jnp.concatenate([*two, side * mine], axis=1))
    across = dot(jnp.concatenate(lefts, axis=0), band_ref[...], NN)
    for m in range(count):
        along = t_ref[at(row + m), :] + t_ref[at(row + m + 2), :]
        if extra is not None and m == extra[0]:
            along = along + extra[1]
        here = across[m // 2 * KA : (m // 2 + 1) * KA, m % 2 * N : (m % 2 + 1) * N]
        s = (here + along) * root_ref[...]
        s_ref[pl.ds(pl.multiple_of((to + m) * KA, 8), KA), :] = s
        square_ref[pl.ds(to + m, 1), :] = jnp.sum(s * s, axis=0, keepdims=True)


def smooth_top_kernel(t_ref, r0, r1, rc, ro, root_ref, band_ref, s_ref, square_ref, side_ref, south_ref):
    north, south, west, east = halos(r0, r1, rc, ro)
    low = iota((KA, N), 1) < 64
    side_ref[...] = jnp.where(low, pltpu.roll(west, 64, 1), east).astype(BF16)
    south_ref[...] = south
    side = jnp.where(low, west, pltpu.roll(east, 64, 1)).astype(BF16)

    def rows(i, _):
        beyond = jnp.where(i == 0, north, 0.0)
        smooth_rows(t_ref, side, root_ref, band_ref, s_ref, square_ref, 32 * i, 32, 32 * i, (0, beyond))
        return 0

    lax.fori_loop(0, 2, rows, 0)
    if TOP > 64:
        smooth_rows(t_ref, side_ref[...], root_ref, band_ref, s_ref, square_ref, 64, TOP - 64, 64)


def smooth_bottom_kernel(t_ref, side_ref, south_ref, root_ref, band_ref, s_ref, square_ref):
    count = (N - TOP) // 2

    def rows(i, _):
        beyond = jnp.where(i == 1, south_ref[...], 0.0)
        row = TOP + count * i
        smooth_rows(t_ref, side_ref[...], root_ref, band_ref, s_ref, square_ref, row, count, count * i, (count - 1, beyond))
        return 0

    lax.fori_loop(0, 2, rows, 0)


def final_kernel(p0, p1, p2, p3, s0_ref, s1_ref, square0, square1, lab_ref, own_ref, root_ref, out_ref, e_ref):
    own = own_ref[...]
    lefts, rights = [], []
    for p in (p0, p1, p2, p3):
        pay = p[...]
        gl = pay[LEV + 2 : LEV + 3].astype(F32) * 64.0 + pay[LEV + 3 : LEV + 4].astype(F32)
        lefts.append(pay)
        rights.append(jnp.where(own == gl, 1.0, 0.0).astype(BF16))
    total = dot(jnp.concatenate(lefts, axis=1), jnp.concatenate(rights, axis=1), NT)
    count = 256.0 * total[LEV : LEV + 1] + 32.0 * total[LEV + 1 : LEV + 2]
    profile = root_ref[...] * (total * (8.0 / jnp.maximum(count, 1.0)))
    hi = profile.astype(BF16).astype(F32)
    lo = (profile - hi).astype(BF16).astype(F32)
    profile = hi + lo
    energy = jnp.sum(profile * profile, axis=0, keepdims=True)
    energy_hi = energy.astype(BF16).astype(F32)
    row = iota((KA, N), 0)
    hi = jnp.where(row == LEV, energy_hi, hi).astype(BF16)
    lo = jnp.where(row == LEV, energy - energy_hi, lo).astype(BF16)
    left = jnp.concatenate([hi, lo], axis=1)
    ids = iota((N, N), 0).astype(F32).astype(BF16)

    def patch_row(q, s_ref, top):
        row = lab_ref[pl.ds(4 * q, 1), :].astype(F32).astype(BF16)
        mark = jnp.where(row == ids, BF16(1.0), BF16(0.0))
        placed = dot(left, jnp.concatenate([mark, mark], axis=0), NN)
        e_ref[pl.ds(4 * q, 4), :] = placed[LEV : LEV + 1] + jnp.zeros((4, N), F32)
        for m in range(4):
            r = 4 * q + m
            cross = s_ref[pl.ds((r - top) * KA, KA), :] * placed
            out_ref[pl.ds(r, 1), :] = jnp.sum(cross, axis=0, keepdims=True)

    for q in range(N // 4):
        if 4 * q < TOP:
            patch_row(q, s0_ref, 0)
        else:
            patch_row(q, s1_ref, TOP)
    e = e_ref[...]
    square = jnp.concatenate([square0[...], square1[...]], axis=0)
    out_ref[...] = jnp.sqrt(jnp.maximum(square - 2.0 * out_ref[...] + e, 0.0) / e)


def vertical(turn):
    pairs = []
    for i in range(8):
        for j in range(16):
            if (j % 4 < 2) == (turn == 0):
                other = 16 * i + (j ^ 1) if i in (0, 7) else 16 * (i + 1 if i % 2 else i - 1) + j
            else:
                other = 16 * (i ^ 1) + j
            pairs.append((16 * i + j, other))
    return pairs


def params(mib):
    return pltpu.CompilerParams(vmem_limit_bytes=mib * 1024 * 1024)


def cost(flops, moved):
    return pl.CostEstimate(flops=flops, bytes_accessed=moved, transcendentals=0)


def shards(humidity, wind_u, wind_v, weights, labels, global_labels):
    vmem = pl.BlockSpec(memory_space=pltpu.VMEM)
    anywhere = pl.BlockSpec(memory_space=pl.ANY)
    edge = pltpu.VMEM((KA, N), BF16)
    wide = pltpu.VMEM((KA, N), F32)
    gl = global_labels.reshape(1, N)
    w = weights.reshape(1, LEV)
    t, s0, s1, c0, c1, band = pl.pallas_call(
        transport_kernel,
        out_shape=(pltpu.VMEM(((N + 2) * KP, N), F32), edge, edge, edge, edge, pltpu.VMEM((3 * N, 2 * N), BF16)),
        in_specs=[anywhere] * 3,
        out_specs=[vmem] * 6,
        scratch_shapes=[pltpu.VMEM((LEV, N, N), BF16)] * 3
        + [pltpu.VMEM((3, N, N), BF16), pltpu.VMEM((N, N), BF16), pltpu.VMEM((2, KA, 3 * N), BF16)]
        + [pltpu.SemaphoreType.DMA((len(CHUNKS), 3))],
        compiler_params=params(18),
        cost_estimate=cost(30_000_000, 23_000_000),
        name="transport",
    )(*(pltpu.with_memory_space_constraint(x, pltpu.HBM) for x in (humidity, wind_u, wind_v)))
    r0 = lax.ppermute(s0, ("lat", "lon"), vertical(0))
    r1 = lax.ppermute(s1, ("lat", "lon"), vertical(1))
    ro = lax.ppermute(c1, "lon", [(j, (j + 1) % 16 if j % 2 else (j - 1) % 16) for j in range(16)])
    rc = lax.ppermute(c0, "lon", [(j, j ^ 1) for j in range(16)])
    t0, root, own, marks = pl.pallas_call(
        sums_kernel,
        out_shape=(wide, wide, pltpu.VMEM((N, N), F32), pltpu.VMEM((N, 4 * N), BF16)),
        in_specs=[vmem] * 4,
        out_specs=[vmem] * 4,
        scratch_shapes=[pltpu.VMEM((N, N), jnp.int32)] * 2,
        compiler_params=params(8),
        cost_estimate=cost(600_000_000, 9_500_000),
        name="sums",
    )(t, labels, gl, w)
    pay = pl.pallas_call(
        pack_kernel,
        out_shape=edge,
        in_specs=[vmem] * 6,
        out_specs=vmem,
        compiler_params=params(8),
        cost_estimate=cost(20_000_000, 300_000),
        name="pack",
    )(t0, r0, r1, ro, rc, marks)
    p2 = lax.ppermute(pay, "lat", [(i, (i + 4) % 8) for i in range(8)])
    p1 = lax.ppermute(pay, "lon", [(j, j ^ 1) for j in range(16)])
    p3 = lax.ppermute(p2, "lon", [(j, j ^ 1) for j in range(16)])
    top0, square0, side, south = pl.pallas_call(
        smooth_top_kernel,
        out_shape=(pltpu.VMEM((TOP * KA, N), F32), pltpu.VMEM((TOP, N), F32), edge, wide),
        in_specs=[vmem] * 7,
        out_specs=[vmem] * 4,
        compiler_params=params(12),
        cost_estimate=cost(600_000_000, 9_500_000),
        name="smooth_top",
    )(t, r0, r1, rc, ro, root, band)
    bottom, square1 = pl.pallas_call(
        smooth_bottom_kernel,
        out_shape=(pltpu.VMEM(((N - TOP) * KA, N), F32), pltpu.VMEM((N - TOP, N), F32)),
        in_specs=[vmem] * 5,
        out_specs=[vmem] * 2,
        compiler_params=params(12),
        cost_estimate=cost(600_000_000, 9_500_000),
        name="smooth_bottom",
    )(t, side, south, root, band)
    return pl.pallas_call(
        final_kernel,
        out_shape=jax.ShapeDtypeStruct((N, N), F32),
        in_specs=[vmem] * 11,
        out_specs=vmem,
        scratch_shapes=[pltpu.VMEM((N, N), F32)],
        compiler_params=params(8),
        cost_estimate=cost(300_000_000, 9_500_000),
        name="final",
    )(pay, p1, p2, p3, top0, bottom, square0, square1, labels, own, root)


def solution(mesh):
    return jax.shard_map(
        shards,
        mesh=mesh,
        in_specs=(
            P(None, "lat", "lon"),
            P(None, "lat", "lon"),
            P(None, "lat", "lon"),
            P(),
            P("lat", "lon"),
            P("lat", "lon", None),
        ),
        out_specs=P("lat", "lon"),
        check_vma=False,
    )
```

```python
import jax
import jax.numpy as jnp
from jax import lax
from jax.experimental import pallas as pl
from jax.experimental.pallas import tpu as pltpu
from jax.sharding import PartitionSpec as P

F32 = jnp.float32
BF16 = jnp.bfloat16
LEV = 137
KA = 144
TOP = 88
KP = 152
N = 128
CHUNKS = ((0, 8), (8, 16), (24, 24), (48, 24), (72, 24), (96, 24), (120, 8), (128, 9))
NT = (((1,), (1,)), ((), ()))
NN = (((1,), (0,)), ((), ()))


def iota(shape, dim):
    return lax.broadcasted_iota(jnp.int32, shape, dim)


def dot(a, b, dims):
    return lax.dot_general(a, b, dims, preferred_element_type=F32)


def column(row, rows):
    shape = (rows, row.shape[1])
    return jnp.sum(jnp.where(iota(shape, 0) == iota(shape, 1), row, 0.0), axis=1, keepdims=True)


def ends():
    shape = (16, N)
    first = (iota(shape, 0) == 0) & (iota(shape, 1) == 0)
    last = (iota(shape, 0) == 1) & (iota(shape, 1) == N - 1)
    return jnp.where(first | last, 1.0, 0.0).astype(BF16)


def north_first():
    i, j = lax.axis_index("lat"), lax.axis_index("lon")
    return (lax.rem(i, 2) == 0) == (lax.rem(j, 4) < 2)


def halos(r0, r1, rc, ro):
    i, j = lax.axis_index("lat"), lax.axis_index("lon")
    first, j_even = north_first(), lax.rem(j, 2) == 0
    r0, r1, rc, ro = (r[...].astype(F32) for r in (r0, r1, rc, ro))
    north = jnp.where(i == 0, 0.0, jnp.where(first, r0, r1))
    south = jnp.where(i == 7, 0.0, jnp.where(first, r1, r0))
    west = jnp.where(j_even, ro, rc)
    east = jnp.where(j_even, rc, ro)
    return north, south, west, east


def transport_kernel(h_hbm, u_hbm, v_hbm, t_ref, s0_ref, s1_ref, c0_ref, c1_ref, band_ref, hb, ub, vb, cols, near, picks, sems):
    copies = []
    for c, (a, n) in enumerate(CHUNKS):
        row = []
        for m, (src, dst) in enumerate(((h_hbm, hb), (u_hbm, ub), (v_hbm, vb))):
            copy = pltpu.make_async_copy(src.at[pl.ds(a, n)], dst.at[pl.ds(a, n)], sems.at[c, m])
            copy.start()
            row.append(copy)
        copies.append(row)
    zeros = jnp.zeros((N, N), F32)
    for k in range(LEV, KA):
        t_ref[pl.ds(KP + k, N, stride=KP), :] = zeros
    blank = jnp.zeros((KA, N), F32)
    t_ref[pl.ds(0, KA), :] = blank
    t_ref[pl.ds((N + 1) * KP, KA), :] = blank
    cols[...] = jnp.zeros((3, N, N), BF16)
    lane = iota((N, N), 1)
    first, j_even = north_first(), lax.rem(lax.axis_index("lon"), 2) == 0
    k, at = iota((KA, 3 * N), 0), iota((KA, 3 * N), 1)
    left_at = 2 * k
    right_at = jnp.where(lax.rem(k, 64) == 0, 2 * k + N - 1, 2 * k - 1)
    picks[0] = jnp.where(at == jnp.where(j_even, right_at, left_at), 1.0, 0.0).astype(BF16)
    picks[1] = jnp.where(at == jnp.where(j_even, left_at, right_at), 1.0, 0.0).astype(BF16)

    a, c = iota((3 * N, 2 * N), 0), iota((3 * N, 2 * N), 1)
    a_in, a_of, c_in, c_of = lax.rem(a, N), lax.div(a, N), lax.rem(c, N), lax.div(c, N)
    band = jnp.where(a_in == c_in, 4.0, jnp.where(jnp.abs(a_in - c_in) == 1, 1.0, 0.0))
    edge = jnp.where(c_in == jnp.where(a_in < 64, 0, N - 1), 1.0, 0.0)
    edge = jnp.where(lax.rem(a, 2) == c_of, edge, 0.0)
    band_ref[...] = jnp.where(a_of == 2, edge, jnp.where(a_of == c_of, band, 0.0)).astype(BF16)

    def level(k):
        parts = []
        for b in range(0, N, 32):
            rows = pl.ds(b, 32)
            u, v = ub[k, rows, :], vb[k, rows, :]
            x = (u * u + v * v).astype(F32) + 1.0
            t = hb[k, rows, :].astype(F32) * (x * lax.rsqrt(x))
            t_ref[pl.ds((1 + b) * KP + k, 32, stride=KP), :] = t
            parts.append(t.astype(BF16))
        return jnp.concatenate(parts, axis=0)

    def group(k, size):
        ends = level(k)
        for q in range(1, size):
            moved = pltpu.roll(level(k + q), 2 * q, 1)
            ends = jnp.where((lane == 2 * q) | (lane == 2 * q - 1), moved, ends)
        near[...] = ends

    def merge(k, size):
        shift = 2 * lax.rem(k, 64)
        mine = lax.rem(lane - shift + N + 1, N) < 2 * size
        block = lax.div(k, 64)
        cols[block] = jnp.where(mine, pltpu.roll(near[...], shift, 1), cols[block])

    for (a, n), row in zip(CHUNKS, copies):
        for copy in row:
            copy.wait()

        def groups(g, _, a=a):
            merge(a + 8 * g - 8, 8)
            group(a + 8 * g, 8)
            return 0

        if a == 0:
            group(0, 8)
        lax.fori_loop(1 if a == 0 else 0, n // 8, groups, 0)
        if n % 8:
            end = a + n - n % 8
            merge(end - 8, 8)
            group(end, n % 8)
            merge(end, n % 8)

    def row_at(top):
        start = pl.multiple_of(jnp.where(top, KP, N * KP), 8)
        return t_ref[pl.ds(start, KA), :].astype(BF16)

    packed = jnp.concatenate([cols[0], cols[1], cols[2]], axis=1)
    s0_ref[...] = row_at(first)
    s1_ref[...] = row_at(jnp.logical_not(first))
    c0_ref[...] = dot(picks[0], packed, NT).astype(BF16)
    c1_ref[...] = dot(picks[1], packed, NT).astype(BF16)


def sums_kernel(t_ref, lab_ref, gl_ref, w_ref, t0_ref, root_ref, own_ref, marks_ref, west_ref, east_ref):
    root_ref[...] = jnp.sqrt(column(w_ref[...], KA)) * 0.125 + jnp.zeros((KA, N), F32)
    own_ref[...] = column(gl_ref[...].astype(F32), N) + jnp.zeros((N, N), F32)
    lab = lab_ref[...]
    lane = iota((N, N), 1)
    west_ref[...] = jnp.where(lane == 0, -1, pltpu.roll(lab, 1, 1))
    east_ref[...] = jnp.where(lane == N - 1, -1, pltpu.roll(lab, N - 1, 1))
    ids = iota((N, N), 0).astype(F32).astype(BF16)
    t0_ref[...] = jnp.zeros((KA, N), F32)
    last = iota((8, N), 0) + (LEV - LEV % 8)

    def patch_row(q):
        base = pl.multiple_of((1 + 4 * q) * KP, 8)
        x = [t_ref[pl.ds(base + m * KP, KA), :] for m in range(-1, 5)]
        whole = x[1] + x[2] + x[3] + x[4]
        step = (x[0] - x[4]) + (x[5] - x[1])
        step = jnp.concatenate([step[: LEV - LEV % 8], jnp.where(last == LEV, 32.0, step[LEV - LEV % 8 :])], axis=0)
        left = jnp.concatenate([whole.astype(BF16), step.astype(BF16)], axis=1)

        def marks(ref):
            row = ref[pl.ds(4 * q, 1), :].astype(F32).astype(BF16)
            return jnp.where(row == ids, BF16(0.125), BF16(0.0))

        here = marks(lab_ref)
        spread = here * BF16(6.0) + (marks(west_ref) + marks(east_ref))
        return left, jnp.concatenate([spread, here], axis=1)

    def patch_rows(i, _):
        pairs = [patch_row(16 * i + m) for m in range(16)]
        left, right = (jnp.concatenate(p, axis=1) for p in zip(*pairs))
        t0_ref[...] += dot(left, right, NT)
        return 0

    lax.fori_loop(0, N // 64, patch_rows, 0)
    total = t0_ref[LEV - LEV % 8 :, :]
    count = total[LEV % 8 : LEV % 8 + 1] * (1.0 / 32.0)
    count_hi = jnp.floor(count * 0.125)
    gl = gl_ref[...].astype(F32)
    gl_hi = jnp.floor(gl * (1.0 / 64.0))
    for m, extra in enumerate((count_hi, count - 8.0 * count_hi, gl_hi, gl - 64.0 * gl_hi)):
        total = jnp.where(last == LEV + m, extra, total)
    t0_ref[LEV - LEV % 8 :, :] = total

    sides = dot(ends(), lab.astype(F32).astype(BF16), NT)
    rows = iota((N, N), 0).astype(F32)

    def edge_marks(row, there):
        return jnp.where((row == rows) & there, 0.125, 0.0)

    i, j = lax.axis_index("lat"), lax.axis_index("lon")
    up, j_even = north_first(), lax.rem(j, 2) == 0
    north = edge_marks(lab[0:1].astype(F32), i > 0)
    south = edge_marks(lab[N - 1 : N].astype(F32), i < 7)
    west, east = edge_marks(sides[0:1], True), edge_marks(sides[1:2], True)
    marks_ref[...] = jnp.concatenate(
        [jnp.where(up, north, south), jnp.where(up, south, north), jnp.where(j_even, west, east), jnp.where(j_even, east, west)],
        axis=1,
    ).astype(BF16)


def pack_kernel(t0_ref, r0, r1, ro, rc, marks_ref, pay_ref):
    left = jnp.concatenate([r0[...], r1[...], ro[...], rc[...]], axis=1)
    pay_ref[...] = (t0_ref[...] + dot(left, marks_ref[...], NT)).astype(BF16)


def smooth_rows(t_ref, side, root_ref, band_ref, s_ref, square_ref, row, count, to, extra=None):
    pair = lax.div(lax.rem(iota((1, N), 1), 64), 2)

    def at(r):
        return pl.ds(pl.multiple_of(r * KP, 8), KA)

    lefts = []
    for m in range(0, count, 2):
        mine = jnp.where(pair == lax.div(lax.rem(row + m, 64), 2), 1.0, 0.0).astype(BF16)
        two = [t_ref[at(row + m + n), :].astype(BF16) for n in (1, 2)]
        lefts.append(jnp.concatenate([*two, side * mine], axis=1))
    across = dot(jnp.concatenate(lefts, axis=0), band_ref[...], NN)
    for m in range(count):
        along = t_ref[at(row + m), :] + t_ref[at(row + m + 2), :]
        if extra is not None and m == extra[0]:
            along = along + extra[1]
        here = across[m // 2 * KA : (m // 2 + 1) * KA, m % 2 * N : (m % 2 + 1) * N]
        s = (here + along) * root_ref[...]
        s_ref[pl.ds(pl.multiple_of((to + m) * KA, 8), KA), :] = s
        square_ref[pl.ds(to + m, 1), :] = jnp.sum(s * s, axis=0, keepdims=True)


def smooth_top_kernel(t_ref, r0, r1, rc, ro, root_ref, band_ref, s_ref, square_ref, side_ref, south_ref):
    north, south, west, east = halos(r0, r1, rc, ro)
    low = iota((KA, N), 1) < 64
    side_ref[...] = jnp.where(low, pltpu.roll(west, 64, 1), east).astype(BF16)
    south_ref[...] = south
    side = jnp.where(low, west, pltpu.roll(east, 64, 1)).astype(BF16)

    def rows(i, _):
        beyond = jnp.where(i == 0, north, 0.0)
        smooth_rows(t_ref, side, root_ref, band_ref, s_ref, square_ref, 32 * i, 32, 32 * i, (0, beyond))
        return 0

    lax.fori_loop(0, 2, rows, 0)
    if TOP > 64:
        smooth_rows(t_ref, side_ref[...], root_ref, band_ref, s_ref, square_ref, 64, TOP - 64, 64)


def smooth_bottom_kernel(t_ref, side_ref, south_ref, root_ref, band_ref, s_ref, square_ref):
    count = (N - TOP) // 2

    def rows(i, _):
        beyond = jnp.where(i == 1, south_ref[...], 0.0)
        row = TOP + count * i
        smooth_rows(t_ref, side_ref[...], root_ref, band_ref, s_ref, square_ref, row, count, count * i, (count - 1, beyond))
        return 0

    lax.fori_loop(0, 2, rows, 0)


def final_kernel(p0, p1, p2, p3, s0_ref, s1_ref, square0, square1, lab_ref, own_ref, root_ref, out_ref, e_ref, cross_ref):
    own = own_ref[...]
    lefts, rights = [], []
    for p in (p0, p1, p2, p3):
        pay = p[...]
        gl = pay[LEV + 2 : LEV + 3].astype(F32) * 64.0 + pay[LEV + 3 : LEV + 4].astype(F32)
        lefts.append(pay)
        rights.append(jnp.where(own == gl, 1.0, 0.0).astype(BF16))
    total = dot(jnp.concatenate(lefts, axis=1), jnp.concatenate(rights, axis=1), NT)
    count = 256.0 * total[LEV : LEV + 1] + 32.0 * total[LEV + 1 : LEV + 2]
    profile = root_ref[...] * (total * (8.0 / jnp.maximum(count, 1.0)))
    hi = profile.astype(BF16).astype(F32)
    lo = (profile - hi).astype(BF16).astype(F32)
    profile = hi + lo
    energy = jnp.sum(profile * profile, axis=0, keepdims=True)
    energy_hi = energy.astype(BF16).astype(F32)
    row = iota((KA, N), 0)
    hi = jnp.where(row == LEV, energy_hi, hi).astype(BF16)
    lo = jnp.where(row == LEV, energy - energy_hi, lo).astype(BF16)
    left = jnp.concatenate([hi, lo], axis=1)
    ids = iota((N, N), 0).astype(F32).astype(BF16)

    def patch_row(q, s_ref, top):
        row = lab_ref[pl.ds(4 * q, 1), :].astype(F32).astype(BF16)
        mark = jnp.where(row == ids, BF16(1.0), BF16(0.0))
        placed = dot(left, jnp.concatenate([mark, mark], axis=0), NN)
        e_ref[pl.ds(4 * q, 4), :] = placed[LEV : LEV + 1] + jnp.zeros((4, N), F32)
        for m in range(4):
            r = 4 * q + m
            cross = s_ref[pl.ds((r - top) * KA, KA), :] * placed
            cross_ref[pl.ds(8 * r, 8), :] = jnp.sum(cross.reshape(KA // 8, 8, N), axis=0)

    for q in range(N // 4):
        if 4 * q < TOP:
            patch_row(q, s0_ref, 0)
        else:
            patch_row(q, s1_ref, TOP)
    e = e_ref[...]
    square = jnp.concatenate([square0[...], square1[...]], axis=0)
    cross = sum(cross_ref[pl.ds(m, N, stride=8), :] for m in range(8))
    out_ref[...] = jnp.sqrt(jnp.maximum(square - 2.0 * cross + e, 0.0) / e)


def vertical(turn):
    pairs = []
    for i in range(8):
        for j in range(16):
            if (j % 4 < 2) == (turn == 0):
                other = 16 * i + (j ^ 1) if i in (0, 7) else 16 * (i + 1 if i % 2 else i - 1) + j
            else:
                other = 16 * (i ^ 1) + j
            pairs.append((16 * i + j, other))
    return pairs


def params(mib):
    return pltpu.CompilerParams(vmem_limit_bytes=mib * 1024 * 1024)


def cost(flops, moved):
    return pl.CostEstimate(flops=flops, bytes_accessed=moved, transcendentals=0)


def shards(humidity, wind_u, wind_v, weights, labels, global_labels):
    vmem = pl.BlockSpec(memory_space=pltpu.VMEM)
    anywhere = pl.BlockSpec(memory_space=pl.ANY)
    edge = pltpu.VMEM((KA, N), BF16)
    wide = pltpu.VMEM((KA, N), F32)
    gl = global_labels.reshape(1, N)
    w = weights.reshape(1, LEV)
    t, s0, s1, c0, c1, band = pl.pallas_call(
        transport_kernel,
        out_shape=(pltpu.VMEM(((N + 2) * KP, N), F32), edge, edge, edge, edge, pltpu.VMEM((3 * N, 2 * N), BF16)),
        in_specs=[anywhere] * 3,
        out_specs=[vmem] * 6,
        scratch_shapes=[pltpu.VMEM((LEV, N, N), BF16)] * 3
        + [pltpu.VMEM((3, N, N), BF16), pltpu.VMEM((N, N), BF16), pltpu.VMEM((2, KA, 3 * N), BF16)]
        + [pltpu.SemaphoreType.DMA((len(CHUNKS), 3))],
        compiler_params=params(18),
        cost_estimate=cost(30_000_000, 23_000_000),
        name="transport",
    )(*(pltpu.with_memory_space_constraint(x, pltpu.HBM) for x in (humidity, wind_u, wind_v)))
    r0 = lax.ppermute(s0, ("lat", "lon"), vertical(0))
    r1 = lax.ppermute(s1, ("lat", "lon"), vertical(1))
    ro = lax.ppermute(c1, "lon", [(j, (j + 1) % 16 if j % 2 else (j - 1) % 16) for j in range(16)])
    rc = lax.ppermute(c0, "lon", [(j, j ^ 1) for j in range(16)])
    t0, root, own, marks = pl.pallas_call(
        sums_kernel,
        out_shape=(wide, wide, pltpu.VMEM((N, N), F32), pltpu.VMEM((N, 4 * N), BF16)),
        in_specs=[vmem] * 4,
        out_specs=[vmem] * 4,
        scratch_shapes=[pltpu.VMEM((N, N), jnp.int32)] * 2,
        compiler_params=params(8),
        cost_estimate=cost(600_000_000, 9_500_000),
        name="sums",
    )(t, labels, gl, w)
    pay = pl.pallas_call(
        pack_kernel,
        out_shape=edge,
        in_specs=[vmem] * 6,
        out_specs=vmem,
        compiler_params=params(8),
        cost_estimate=cost(20_000_000, 300_000),
        name="pack",
    )(t0, r0, r1, ro, rc, marks)
    p2 = lax.ppermute(pay, "lat", [(i, (i + 4) % 8) for i in range(8)])
    p1 = lax.ppermute(pay, "lon", [(j, j ^ 1) for j in range(16)])
    p3 = lax.ppermute(p2, "lon", [(j, j ^ 1) for j in range(16)])
    top0, square0, side, south = pl.pallas_call(
        smooth_top_kernel,
        out_shape=(pltpu.VMEM((TOP * KA, N), F32), pltpu.VMEM((TOP, N), F32), edge, wide),
        in_specs=[vmem] * 7,
        out_specs=[vmem] * 4,
        compiler_params=params(12),
        cost_estimate=cost(600_000_000, 9_500_000),
        name="smooth_top",
    )(t, r0, r1, rc, ro, root, band)
    bottom, square1 = pl.pallas_call(
        smooth_bottom_kernel,
        out_shape=(pltpu.VMEM(((N - TOP) * KA, N), F32), pltpu.VMEM((N - TOP, N), F32)),
        in_specs=[vmem] * 5,
        out_specs=[vmem] * 2,
        compiler_params=params(12),
        cost_estimate=cost(600_000_000, 9_500_000),
        name="smooth_bottom",
    )(t, side, south, root, band)
    return pl.pallas_call(
        final_kernel,
        out_shape=jax.ShapeDtypeStruct((N, N), F32),
        in_specs=[vmem] * 11,
        out_specs=vmem,
        scratch_shapes=[pltpu.VMEM((N, N), F32), pltpu.VMEM((8 * N, N), F32)],
        compiler_params=params(8),
        cost_estimate=cost(300_000_000, 9_500_000),
        name="final",
    )(pay, p1, p2, p3, top0, bottom, square0, square1, labels, own, root)


def solution(mesh):
    return jax.shard_map(
        shards,
        mesh=mesh,
        in_specs=(
            P(None, "lat", "lon"),
            P(None, "lat", "lon"),
            P(None, "lat", "lon"),
            P(),
            P("lat", "lon"),
            P("lat", "lon", None),
        ),
        out_specs=P("lat", "lon"),
        check_vma=False,
    )
```

```python
import jax
import jax.numpy as jnp
from jax import lax
from jax.experimental import pallas as pl
from jax.experimental.pallas import tpu as pltpu
from jax.sharding import PartitionSpec as P

F32 = jnp.float32
BF16 = jnp.bfloat16
LEV = 137
KA = 144
TOP = 88
KP = 152
N = 128
CHUNKS = ((0, 8), (8, 16), (24, 24), (48, 24), (72, 24), (96, 24), (120, 8), (128, 9))
NT = (((1,), (1,)), ((), ()))
NN = (((1,), (0,)), ((), ()))


def iota(shape, dim):
    return lax.broadcasted_iota(jnp.int32, shape, dim)


def dot(a, b, dims):
    return lax.dot_general(a, b, dims, preferred_element_type=F32)


def column(row, rows):
    shape = (rows, row.shape[1])
    return jnp.sum(jnp.where(iota(shape, 0) == iota(shape, 1), row, 0.0), axis=1, keepdims=True)


def ends():
    shape = (16, N)
    first = (iota(shape, 0) == 0) & (iota(shape, 1) == 0)
    last = (iota(shape, 0) == 1) & (iota(shape, 1) == N - 1)
    return jnp.where(first | last, 1.0, 0.0).astype(BF16)


def north_first():
    i, j = lax.axis_index("lat"), lax.axis_index("lon")
    return (lax.rem(i, 2) == 0) == (lax.rem(j, 4) < 2)


def halos(r0, r1, rc, ro):
    i, j = lax.axis_index("lat"), lax.axis_index("lon")
    first, j_even = north_first(), lax.rem(j, 2) == 0
    r0, r1, rc, ro = (r[...].astype(F32) for r in (r0, r1, rc, ro))
    north = jnp.where(i == 0, 0.0, jnp.where(first, r0, r1))
    south = jnp.where(i == 7, 0.0, jnp.where(first, r1, r0))
    west = jnp.where(j_even, ro, rc)
    east = jnp.where(j_even, rc, ro)
    return north, south, west, east


def transport_kernel(h_hbm, u_hbm, v_hbm, t_ref, s0_ref, s1_ref, c0_ref, c1_ref, band_ref, hb, ub, vb, cols, near, picks, sems):
    copies = []
    for c, (a, n) in enumerate(CHUNKS):
        row = []
        for m, (src, dst) in enumerate(((h_hbm, hb), (u_hbm, ub), (v_hbm, vb))):
            copy = pltpu.make_async_copy(src.at[pl.ds(a, n)], dst.at[pl.ds(a, n)], sems.at[c, m])
            copy.start()
            row.append(copy)
        copies.append(row)
    zeros = jnp.zeros((N, N), F32)
    for k in range(LEV, KA):
        t_ref[pl.ds(KP + k, N, stride=KP), :] = zeros
    blank = jnp.zeros((KA, N), F32)
    t_ref[pl.ds(0, KA), :] = blank
    t_ref[pl.ds((N + 1) * KP, KA), :] = blank
    cols[...] = jnp.zeros((3, N, N), BF16)
    lane = iota((N, N), 1)
    first, j_even = north_first(), lax.rem(lax.axis_index("lon"), 2) == 0
    k, at = iota((KA, 3 * N), 0), iota((KA, 3 * N), 1)
    left_at = 2 * k
    right_at = jnp.where(lax.rem(k, 64) == 0, 2 * k + N - 1, 2 * k - 1)
    picks[0] = jnp.where(at == jnp.where(j_even, right_at, left_at), 1.0, 0.0).astype(BF16)
    picks[1] = jnp.where(at == jnp.where(j_even, left_at, right_at), 1.0, 0.0).astype(BF16)

    a, c = iota((3 * N, 2 * N), 0), iota((3 * N, 2 * N), 1)
    a_in, a_of, c_in, c_of = lax.rem(a, N), lax.div(a, N), lax.rem(c, N), lax.div(c, N)
    band = jnp.where(a_in == c_in, 4.0, jnp.where(jnp.abs(a_in - c_in) == 1, 1.0, 0.0))
    edge = jnp.where(c_in == jnp.where(a_in < 64, 0, N - 1), 1.0, 0.0)
    edge = jnp.where(lax.rem(a, 2) == c_of, edge, 0.0)
    band_ref[...] = jnp.where(a_of == 2, edge, jnp.where(a_of == c_of, band, 0.0)).astype(BF16)

    def level(k):
        parts = []
        for b in range(0, N, 32):
            rows = pl.ds(b, 32)
            u, v = ub[k, rows, :], vb[k, rows, :]
            x = (u * u + v * v).astype(F32) + 1.0
            t = hb[k, rows, :].astype(F32) * (x * lax.rsqrt(x))
            t_ref[pl.ds((1 + b) * KP + k, 32, stride=KP), :] = t
            parts.append(t.astype(BF16))
        return jnp.concatenate(parts, axis=0)

    def group(k, size):
        ends = level(k)
        for q in range(1, size):
            moved = pltpu.roll(level(k + q), 2 * q, 1)
            ends = jnp.where((lane == 2 * q) | (lane == 2 * q - 1), moved, ends)
        near[...] = ends

    def merge(k, size):
        shift = 2 * lax.rem(k, 64)
        mine = lax.rem(lane - shift + N + 1, N) < 2 * size
        block = lax.div(k, 64)
        cols[block] = jnp.where(mine, pltpu.roll(near[...], shift, 1), cols[block])

    for (a, n), row in zip(CHUNKS, copies):
        for copy in row:
            copy.wait()

        def groups(g, _, a=a):
            merge(a + 8 * g - 8, 8)
            group(a + 8 * g, 8)
            return 0

        if a == 0:
            group(0, 8)
        lax.fori_loop(1 if a == 0 else 0, n // 8, groups, 0)
        if n % 8:
            end = a + n - n % 8
            merge(end - 8, 8)
            group(end, n % 8)
            merge(end, n % 8)

    def row_at(top):
        start = pl.multiple_of(jnp.where(top, KP, N * KP), 8)
        return t_ref[pl.ds(start, KA), :].astype(BF16)

    packed = jnp.concatenate([cols[0], cols[1], cols[2]], axis=1)
    s0_ref[...] = row_at(first)
    s1_ref[...] = row_at(jnp.logical_not(first))
    c0_ref[...] = dot(picks[0], packed, NT).astype(BF16)
    c1_ref[...] = dot(picks[1], packed, NT).astype(BF16)


def sums_kernel(t_ref, lab_ref, gl_ref, w_ref, t0_ref, root_ref, own_ref, marks_ref, west_ref, east_ref):
    root_ref[...] = jnp.sqrt(column(w_ref[...], KA)) * 0.125 + jnp.zeros((KA, N), F32)
    own_ref[...] = column(gl_ref[...].astype(F32), N) + jnp.zeros((N, N), F32)
    lab = lab_ref[...]
    lane = iota((N, N), 1)
    west_ref[...] = jnp.where(lane == 0, -1, pltpu.roll(lab, 1, 1))
    east_ref[...] = jnp.where(lane == N - 1, -1, pltpu.roll(lab, N - 1, 1))
    ids = iota((N, N), 0).astype(F32).astype(BF16)
    t0_ref[...] = jnp.zeros((KA, N), F32)
    last = iota((8, N), 0) + (LEV - LEV % 8)

    def patch_row(q):
        base = pl.multiple_of((1 + 4 * q) * KP, 8)
        x = [t_ref[pl.ds(base + m * KP, KA), :] for m in range(-1, 5)]
        whole = x[1] + x[2] + x[3] + x[4]
        step = (x[0] - x[4]) + (x[5] - x[1])
        step = jnp.concatenate([step[: LEV - LEV % 8], jnp.where(last == LEV, 32.0, step[LEV - LEV % 8 :])], axis=0)
        left = jnp.concatenate([whole.astype(BF16), step.astype(BF16)], axis=1)

        def marks(ref):
            row = ref[pl.ds(4 * q, 1), :].astype(F32).astype(BF16)
            return jnp.where(row == ids, BF16(0.125), BF16(0.0))

        here = marks(lab_ref)
        spread = here * BF16(6.0) + (marks(west_ref) + marks(east_ref))
        return left, jnp.concatenate([spread, here], axis=1)

    def patch_rows(i, _):
        pairs = [patch_row(16 * i + m) for m in range(16)]
        left, right = (jnp.concatenate(p, axis=1) for p in zip(*pairs))
        t0_ref[...] += dot(left, right, NT)
        return 0

    lax.fori_loop(0, N // 64, patch_rows, 0)
    total = t0_ref[LEV - LEV % 8 :, :]
    count = total[LEV % 8 : LEV % 8 + 1] * (1.0 / 32.0)
    count_hi = jnp.floor(count * 0.125)
    gl = gl_ref[...].astype(F32)
    gl_hi = jnp.floor(gl * (1.0 / 64.0))
    for m, extra in enumerate((count_hi, count - 8.0 * count_hi, gl_hi, gl - 64.0 * gl_hi)):
        total = jnp.where(last == LEV + m, extra, total)
    t0_ref[LEV - LEV % 8 :, :] = total

    sides = dot(ends(), lab.astype(F32).astype(BF16), NT)
    rows = iota((N, N), 0).astype(F32)

    def edge_marks(row, there):
        return jnp.where((row == rows) & there, 0.125, 0.0)

    i, j = lax.axis_index("lat"), lax.axis_index("lon")
    up, j_even = north_first(), lax.rem(j, 2) == 0
    north = edge_marks(lab[0:1].astype(F32), i > 0)
    south = edge_marks(lab[N - 1 : N].astype(F32), i < 7)
    west, east = edge_marks(sides[0:1], True), edge_marks(sides[1:2], True)
    marks_ref[...] = jnp.concatenate(
        [jnp.where(up, north, south), jnp.where(up, south, north), jnp.where(j_even, west, east), jnp.where(j_even, east, west)],
        axis=1,
    ).astype(BF16)


def pack_kernel(t0_ref, r0, r1, ro, rc, marks_ref, pay_ref):
    left = jnp.concatenate([r0[...], r1[...], ro[...], rc[...]], axis=1)
    pay_ref[...] = (t0_ref[...] + dot(left, marks_ref[...], NT)).astype(BF16)


def smooth_rows(t_ref, side, root_ref, band_ref, s_ref, square_ref, row, count, to, extra=None):
    pair = lax.div(lax.rem(iota((1, N), 1), 64), 2)

    def at(r):
        return pl.ds(pl.multiple_of(r * KP, 8), KA)

    lefts = []
    for m in range(0, count, 2):
        mine = jnp.where(pair == lax.div(lax.rem(row + m, 64), 2), 1.0, 0.0).astype(BF16)
        two = [t_ref[at(row + m + n), :].astype(BF16) for n in (1, 2)]
        half = side
        if side.shape[0] > KA:
            half = side[pl.ds(pl.multiple_of(KA * lax.div(row + m, 64), 16), KA), :]
        lefts.append(jnp.concatenate([*two, half * mine], axis=1))
    across = dot(jnp.concatenate(lefts, axis=0), band_ref[...], NN)
    for m in range(count):
        along = t_ref[at(row + m), :] + t_ref[at(row + m + 2), :]
        if extra is not None and m == extra[0]:
            along = along + extra[1]
        here = across[m // 2 * KA : (m // 2 + 1) * KA, m % 2 * N : (m % 2 + 1) * N]
        s = (here + along) * root_ref[...]
        s_ref[pl.ds(pl.multiple_of((to + m) * KA, 8), KA), :] = s
        square_ref[pl.ds(to + m, 1), :] = jnp.sum(s * s, axis=0, keepdims=True)


def smooth_top_kernel(t_ref, r0, r1, rc, ro, root_ref, band_ref, s_ref, square_ref, side_ref, south_ref, sides):
    north, south, west, east = halos(r0, r1, rc, ro)
    low = iota((KA, N), 1) < 64
    side_ref[...] = jnp.where(low, pltpu.roll(west, 64, 1), east).astype(BF16)
    south_ref[...] = south
    side = jnp.where(low, west, pltpu.roll(east, 64, 1)).astype(BF16)

    sides[pl.ds(0, KA), :] = side
    sides[pl.ds(KA, KA), :] = side_ref[...]
    count = TOP // 2

    def rows(i, _):
        beyond = jnp.where(i == 0, north, 0.0)
        smooth_rows(t_ref, sides, root_ref, band_ref, s_ref, square_ref, count * i, count, count * i, (0, beyond))
        return 0

    lax.fori_loop(0, 2, rows, 0)


def smooth_bottom_kernel(t_ref, side_ref, south_ref, root_ref, band_ref, s_ref, square_ref):
    count = (N - TOP) // 2

    def rows(i, _):
        beyond = jnp.where(i == 1, south_ref[...], 0.0)
        row = TOP + count * i
        smooth_rows(t_ref, side_ref[...], root_ref, band_ref, s_ref, square_ref, row, count, count * i, (count - 1, beyond))
        return 0

    lax.fori_loop(0, 2, rows, 0)


def final_kernel(p0, p1, p2, p3, s0_ref, s1_ref, square0, square1, lab_ref, own_ref, root_ref, out_ref, e_ref, cross_ref):
    own = own_ref[...]
    lefts, rights = [], []
    for p in (p0, p1, p2, p3):
        pay = p[...]
        gl = pay[LEV + 2 : LEV + 3].astype(F32) * 64.0 + pay[LEV + 3 : LEV + 4].astype(F32)
        lefts.append(pay)
        rights.append(jnp.where(own == gl, 1.0, 0.0).astype(BF16))
    total = dot(jnp.concatenate(lefts, axis=1), jnp.concatenate(rights, axis=1), NT)
    count = 256.0 * total[LEV : LEV + 1] + 32.0 * total[LEV + 1 : LEV + 2]
    profile = root_ref[...] * (total * (8.0 / jnp.maximum(count, 1.0)))
    hi = profile.astype(BF16).astype(F32)
    lo = (profile - hi).astype(BF16).astype(F32)
    profile = hi + lo
    energy = jnp.sum(profile * profile, axis=0, keepdims=True)
    energy_hi = energy.astype(BF16).astype(F32)
    row = iota((KA, N), 0)
    hi = jnp.where(row == LEV, energy_hi, hi).astype(BF16)
    lo = jnp.where(row == LEV, energy - energy_hi, lo).astype(BF16)
    left = jnp.concatenate([hi, lo], axis=1)
    ids = iota((N, N), 0).astype(F32).astype(BF16)

    def patch_row(q, s_ref, top):
        row = lab_ref[pl.ds(4 * q, 1), :].astype(F32).astype(BF16)
        mark = jnp.where(row == ids, BF16(1.0), BF16(0.0))
        placed = dot(left, jnp.concatenate([mark, mark], axis=0), NN)
        e_ref[pl.ds(4 * q, 4), :] = placed[LEV : LEV + 1] + jnp.zeros((4, N), F32)
        for m in range(4):
            r = 4 * q + m
            cross = s_ref[pl.ds((r - top) * KA, KA), :] * placed
            cross_ref[pl.ds(8 * r, 8), :] = jnp.sum(cross.reshape(KA // 8, 8, N), axis=0)

    for q in range(N // 4):
        if 4 * q < TOP:
            patch_row(q, s0_ref, 0)
        else:
            patch_row(q, s1_ref, TOP)
    e = e_ref[...]
    square = jnp.concatenate([square0[...], square1[...]], axis=0)
    cross = sum(cross_ref[pl.ds(m, N, stride=8), :] for m in range(8))
    out_ref[...] = jnp.sqrt(jnp.maximum(square - 2.0 * cross + e, 0.0) / e)


def vertical(turn):
    pairs = []
    for i in range(8):
        for j in range(16):
            if (j % 4 < 2) == (turn == 0):
                other = 16 * i + (j ^ 1) if i in (0, 7) else 16 * (i + 1 if i % 2 else i - 1) + j
            else:
                other = 16 * (i ^ 1) + j
            pairs.append((16 * i + j, other))
    return pairs


def params(mib):
    return pltpu.CompilerParams(vmem_limit_bytes=mib * 1024 * 1024)


def cost(flops, moved):
    return pl.CostEstimate(flops=flops, bytes_accessed=moved, transcendentals=0)


def shards(humidity, wind_u, wind_v, weights, labels, global_labels):
    vmem = pl.BlockSpec(memory_space=pltpu.VMEM)
    anywhere = pl.BlockSpec(memory_space=pl.ANY)
    edge = pltpu.VMEM((KA, N), BF16)
    wide = pltpu.VMEM((KA, N), F32)
    gl = global_labels.reshape(1, N)
    w = weights.reshape(1, LEV)
    t, s0, s1, c0, c1, band = pl.pallas_call(
        transport_kernel,
        out_shape=(pltpu.VMEM(((N + 2) * KP, N), F32), edge, edge, edge, edge, pltpu.VMEM((3 * N, 2 * N), BF16)),
        in_specs=[anywhere] * 3,
        out_specs=[vmem] * 6,
        scratch_shapes=[pltpu.VMEM((LEV, N, N), BF16)] * 3
        + [pltpu.VMEM((3, N, N), BF16), pltpu.VMEM((N, N), BF16), pltpu.VMEM((2, KA, 3 * N), BF16)]
        + [pltpu.SemaphoreType.DMA((len(CHUNKS), 3))],
        compiler_params=params(18),
        cost_estimate=cost(30_000_000, 23_000_000),
        name="transport",
    )(*(pltpu.with_memory_space_constraint(x, pltpu.HBM) for x in (humidity, wind_u, wind_v)))
    r0 = lax.ppermute(s0, ("lat", "lon"), vertical(0))
    r1 = lax.ppermute(s1, ("lat", "lon"), vertical(1))
    ro = lax.ppermute(c1, "lon", [(j, (j + 1) % 16 if j % 2 else (j - 1) % 16) for j in range(16)])
    rc = lax.ppermute(c0, "lon", [(j, j ^ 1) for j in range(16)])
    t0, root, own, marks = pl.pallas_call(
        sums_kernel,
        out_shape=(wide, wide, pltpu.VMEM((N, N), F32), pltpu.VMEM((N, 4 * N), BF16)),
        in_specs=[vmem] * 4,
        out_specs=[vmem] * 4,
        scratch_shapes=[pltpu.VMEM((N, N), jnp.int32)] * 2,
        compiler_params=params(8),
        cost_estimate=cost(600_000_000, 9_500_000),
        name="sums",
    )(t, labels, gl, w)
    pay = pl.pallas_call(
        pack_kernel,
        out_shape=edge,
        in_specs=[vmem] * 6,
        out_specs=vmem,
        compiler_params=params(8),
        cost_estimate=cost(20_000_000, 300_000),
        name="pack",
    )(t0, r0, r1, ro, rc, marks)
    p2 = lax.ppermute(pay, "lat", [(i, (i + 4) % 8) for i in range(8)])
    p1 = lax.ppermute(pay, "lon", [(j, j ^ 1) for j in range(16)])
    p3 = lax.ppermute(p2, "lon", [(j, j ^ 1) for j in range(16)])
    top0, square0, side, south = pl.pallas_call(
        smooth_top_kernel,
        out_shape=(pltpu.VMEM((TOP * KA, N), F32), pltpu.VMEM((TOP, N), F32), edge, wide),
        in_specs=[vmem] * 7,
        out_specs=[vmem] * 4,
        scratch_shapes=[pltpu.VMEM((2 * KA, N), BF16)],
        compiler_params=params(12),
        cost_estimate=cost(600_000_000, 9_500_000),
        name="smooth_top",
    )(t, r0, r1, rc, ro, root, band)
    bottom, square1 = pl.pallas_call(
        smooth_bottom_kernel,
        out_shape=(pltpu.VMEM(((N - TOP) * KA, N), F32), pltpu.VMEM((N - TOP, N), F32)),
        in_specs=[vmem] * 5,
        out_specs=[vmem] * 2,
        compiler_params=params(12),
        cost_estimate=cost(600_000_000, 9_500_000),
        name="smooth_bottom",
    )(t, side, south, root, band)
    return pl.pallas_call(
        final_kernel,
        out_shape=jax.ShapeDtypeStruct((N, N), F32),
        in_specs=[vmem] * 11,
        out_specs=vmem,
        scratch_shapes=[pltpu.VMEM((N, N), F32), pltpu.VMEM((8 * N, N), F32)],
        compiler_params=params(8),
        cost_estimate=cost(300_000_000, 9_500_000),
        name="final",
    )(pay, p1, p2, p3, top0, bottom, square0, square1, labels, own, root)


def solution(mesh):
    return jax.shard_map(
        shards,
        mesh=mesh,
        in_specs=(
            P(None, "lat", "lon"),
            P(None, "lat", "lon"),
            P(None, "lat", "lon"),
            P(),
            P("lat", "lon"),
            P("lat", "lon", None),
        ),
        out_specs=P("lat", "lon"),
        check_vma=False,
    )
```

```python
import jax
import jax.numpy as jnp
from jax import lax
from jax.experimental import pallas as pl
from jax.experimental.pallas import tpu as pltpu
from jax.sharding import PartitionSpec as P

F32 = jnp.float32
BF16 = jnp.bfloat16
LEV = 137
KA = 144
TOP = 88
KP = 152
N = 128
CHUNKS = ((0, 8), (8, 16), (24, 24), (48, 24), (72, 24), (96, 24), (120, 8), (128, 9))
NT = (((1,), (1,)), ((), ()))
NN = (((1,), (0,)), ((), ()))


def iota(shape, dim):
    return lax.broadcasted_iota(jnp.int32, shape, dim)


def dot(a, b, dims):
    return lax.dot_general(a, b, dims, preferred_element_type=F32)


def column(row, rows):
    shape = (rows, row.shape[1])
    return jnp.sum(jnp.where(iota(shape, 0) == iota(shape, 1), row, 0.0), axis=1, keepdims=True)


def ends():
    shape = (16, N)
    first = (iota(shape, 0) == 0) & (iota(shape, 1) == 0)
    last = (iota(shape, 0) == 1) & (iota(shape, 1) == N - 1)
    return jnp.where(first | last, 1.0, 0.0).astype(BF16)


def north_first():
    i, j = lax.axis_index("lat"), lax.axis_index("lon")
    return (lax.rem(i, 2) == 0) == (lax.rem(j, 4) < 2)


def halos(r0, r1, rc, ro):
    i, j = lax.axis_index("lat"), lax.axis_index("lon")
    first, j_even = north_first(), lax.rem(j, 2) == 0
    r0, r1, rc, ro = (r[...].astype(F32) for r in (r0, r1, rc, ro))
    north = jnp.where(i == 0, 0.0, jnp.where(first, r0, r1))
    south = jnp.where(i == 7, 0.0, jnp.where(first, r1, r0))
    west = jnp.where(j_even, ro, rc)
    east = jnp.where(j_even, rc, ro)
    return north, south, west, east


def transport_kernel(h_hbm, u_hbm, v_hbm, t_ref, s0_ref, s1_ref, c0_ref, c1_ref, band_ref, hb, ub, vb, cols, near, picks, sems):
    copies = []
    for c, (a, n) in enumerate(CHUNKS):
        row = []
        for m, (src, dst) in enumerate(((h_hbm, hb), (u_hbm, ub), (v_hbm, vb))):
            copy = pltpu.make_async_copy(src.at[pl.ds(a, n)], dst.at[pl.ds(a, n)], sems.at[c, m])
            copy.start()
            row.append(copy)
        copies.append(row)
    zeros = jnp.zeros((N, N), F32)
    for k in range(LEV, KA):
        t_ref[pl.ds(KP + k, N, stride=KP), :] = zeros
    blank = jnp.zeros((KA, N), F32)
    t_ref[pl.ds(0, KA), :] = blank
    t_ref[pl.ds((N + 1) * KP, KA), :] = blank
    cols[...] = jnp.zeros((3, N, N), BF16)
    lane = iota((N, N), 1)
    first, j_even = north_first(), lax.rem(lax.axis_index("lon"), 2) == 0
    k, at = iota((KA, 3 * N), 0), iota((KA, 3 * N), 1)
    left_at = 2 * k
    right_at = jnp.where(lax.rem(k, 64) == 0, 2 * k + N - 1, 2 * k - 1)
    picks[0] = jnp.where(at == jnp.where(j_even, right_at, left_at), 1.0, 0.0).astype(BF16)
    picks[1] = jnp.where(at == jnp.where(j_even, left_at, right_at), 1.0, 0.0).astype(BF16)

    a, c = iota((3 * N, 2 * N), 0), iota((3 * N, 2 * N), 1)
    a_in, a_of, c_in, c_of = lax.rem(a, N), lax.div(a, N), lax.rem(c, N), lax.div(c, N)
    band = jnp.where(a_in == c_in, 4.0, jnp.where(jnp.abs(a_in - c_in) == 1, 1.0, 0.0))
    edge = jnp.where(c_in == jnp.where(a_in < 64, 0, N - 1), 1.0, 0.0)
    edge = jnp.where(lax.rem(a, 2) == c_of, edge, 0.0)
    band_ref[...] = jnp.where(a_of == 2, edge, jnp.where(a_of == c_of, band, 0.0)).astype(BF16)

    def level(k):
        parts = []
        for b in range(0, N, 32):
            rows = pl.ds(b, 32)
            u, v = ub[k, rows, :], vb[k, rows, :]
            x = (u * u + v * v).astype(F32) + 1.0
            t = hb[k, rows, :].astype(F32) * (x * lax.rsqrt(x))
            t_ref[pl.ds((1 + b) * KP + k, 32, stride=KP), :] = t
            parts.append(t.astype(BF16))
        return jnp.concatenate(parts, axis=0)

    def group(k, size):
        ends = level(k)
        for q in range(1, size):
            moved = pltpu.roll(level(k + q), 2 * q, 1)
            ends = jnp.where((lane == 2 * q) | (lane == 2 * q - 1), moved, ends)
        near[...] = ends

    def merge(k, size):
        shift = 2 * lax.rem(k, 64)
        mine = lax.rem(lane - shift + N + 1, N) < 2 * size
        block = lax.div(k, 64)
        cols[block] = jnp.where(mine, pltpu.roll(near[...], shift, 1), cols[block])

    for (a, n), row in zip(CHUNKS, copies):
        for copy in row:
            copy.wait()

        def groups(g, _, a=a):
            merge(a + 8 * g - 8, 8)
            group(a + 8 * g, 8)
            return 0

        if a == 0:
            group(0, 8)
        lax.fori_loop(1 if a == 0 else 0, n // 8, groups, 0)
        if n % 8:
            end = a + n - n % 8
            merge(end - 8, 8)
            group(end, n % 8)
            merge(end, n % 8)

    def row_at(top):
        start = pl.multiple_of(jnp.where(top, KP, N * KP), 8)
        return t_ref[pl.ds(start, KA), :].astype(BF16)

    packed = jnp.concatenate([cols[0], cols[1], cols[2]], axis=1)
    s0_ref[...] = row_at(first)
    s1_ref[...] = row_at(jnp.logical_not(first))
    c0_ref[...] = dot(picks[0], packed, NT).astype(BF16)
    c1_ref[...] = dot(picks[1], packed, NT).astype(BF16)


def sums_kernel(t_ref, lab_ref, gl_ref, w_ref, t0_ref, root_ref, own_ref, marks_ref, west_ref, east_ref):
    root_ref[...] = jnp.sqrt(column(w_ref[...], KA)) * 0.125 + jnp.zeros((KA, N), F32)
    own_ref[...] = column(gl_ref[...].astype(F32), N) + jnp.zeros((N, N), F32)
    lab = lab_ref[...]
    lane = iota((N, N), 1)
    west_ref[...] = jnp.where(lane == 0, -1, pltpu.roll(lab, 1, 1))
    east_ref[...] = jnp.where(lane == N - 1, -1, pltpu.roll(lab, N - 1, 1))
    ids = iota((N, N), 0).astype(F32).astype(BF16)
    t0_ref[...] = jnp.zeros((KA, N), F32)
    last = iota((8, N), 0) + (LEV - LEV % 8)

    def patch_row(q):
        base = pl.multiple_of((1 + 4 * q) * KP, 8)
        x = [t_ref[pl.ds(base + m * KP, KA), :] for m in range(-1, 5)]
        whole = x[1] + x[2] + x[3] + x[4]
        step = (x[0] - x[4]) + (x[5] - x[1])
        step = jnp.concatenate([step[: LEV - LEV % 8], jnp.where(last == LEV, 32.0, step[LEV - LEV % 8 :])], axis=0)
        left = jnp.concatenate([whole.astype(BF16), step.astype(BF16)], axis=1)

        def marks(ref):
            row = ref[pl.ds(4 * q, 1), :].astype(F32).astype(BF16)
            return jnp.where(row == ids, BF16(0.125), BF16(0.0))

        here = marks(lab_ref)
        spread = here * BF16(6.0) + (marks(west_ref) + marks(east_ref))
        return left, jnp.concatenate([spread, here], axis=1)

    def patch_rows(i, _):
        pairs = [patch_row(16 * i + m) for m in range(16)]
        left, right = (jnp.concatenate(p, axis=1) for p in zip(*pairs))
        t0_ref[...] += dot(left, right, NT)
        return 0

    lax.fori_loop(0, N // 64, patch_rows, 0)
    total = t0_ref[LEV - LEV % 8 :, :]
    count = total[LEV % 8 : LEV % 8 + 1] * (1.0 / 32.0)
    count_hi = jnp.floor(count * 0.125)
    gl = gl_ref[...].astype(F32)
    gl_hi = jnp.floor(gl * (1.0 / 64.0))
    for m, extra in enumerate((count_hi, count - 8.0 * count_hi, gl_hi, gl - 64.0 * gl_hi)):
        total = jnp.where(last == LEV + m, extra, total)
    t0_ref[LEV - LEV % 8 :, :] = total

    sides = dot(ends(), lab.astype(F32).astype(BF16), NT)
    rows = iota((N, N), 0).astype(F32)

    def edge_marks(row, there):
        return jnp.where((row == rows) & there, 0.125, 0.0)

    i, j = lax.axis_index("lat"), lax.axis_index("lon")
    up, j_even = north_first(), lax.rem(j, 2) == 0
    north = edge_marks(lab[0:1].astype(F32), i > 0)
    south = edge_marks(lab[N - 1 : N].astype(F32), i < 7)
    west, east = edge_marks(sides[0:1], True), edge_marks(sides[1:2], True)
    marks_ref[...] = jnp.concatenate(
        [jnp.where(up, north, south), jnp.where(up, south, north), jnp.where(j_even, west, east), jnp.where(j_even, east, west)],
        axis=1,
    ).astype(BF16)


def pack_kernel(t0_ref, r0, r1, ro, rc, marks_ref, pay_ref):
    left = jnp.concatenate([r0[...], r1[...], ro[...], rc[...]], axis=1)
    pay_ref[...] = (t0_ref[...] + dot(left, marks_ref[...], NT)).astype(BF16)


def smooth_rows(t_ref, side, root_ref, band_ref, s_ref, square_ref, row, count, to, extra=None):
    pair = lax.div(lax.rem(iota((1, N), 1), 64), 2)

    def at(r):
        return pl.ds(pl.multiple_of(r * KP, 8), KA)

    lefts = []
    for m in range(0, count, 2):
        mine = jnp.where(pair == lax.div(lax.rem(row + m, 64), 2), 1.0, 0.0).astype(BF16)
        two = [t_ref[at(row + m + n), :].astype(BF16) for n in (1, 2)]
        half = side
        if side.shape[0] > KA:
            half = side[pl.ds(pl.multiple_of(KA * lax.div(row + m, 64), 16), KA), :]
        lefts.append(jnp.concatenate([*two, half * mine], axis=1))
    across = dot(jnp.concatenate(lefts, axis=0), band_ref[...], NN)
    for m in range(count):
        along = t_ref[at(row + m), :] + t_ref[at(row + m + 2), :]
        if extra is not None and m == extra[0]:
            along = along + extra[1]
        here = across[m // 2 * KA : (m // 2 + 1) * KA, m % 2 * N : (m % 2 + 1) * N]
        s = (here + along) * root_ref[...]
        s_ref[pl.ds(pl.multiple_of((to + m) * KA, 8), KA), :] = s
        square_ref[pl.ds(pl.multiple_of(8 * (to + m), 8), 8), :] = jnp.sum((s * s).reshape(KA // 8, 8, N), axis=0)


def smooth_top_kernel(t_ref, r0, r1, rc, ro, root_ref, band_ref, s_ref, square_ref, side_ref, south_ref, sides, parts):
    north, south, west, east = halos(r0, r1, rc, ro)
    low = iota((KA, N), 1) < 64
    side_ref[...] = jnp.where(low, pltpu.roll(west, 64, 1), east).astype(BF16)
    south_ref[...] = south
    side = jnp.where(low, west, pltpu.roll(east, 64, 1)).astype(BF16)

    sides[pl.ds(0, KA), :] = side
    sides[pl.ds(KA, KA), :] = side_ref[...]
    count = TOP // 2

    def rows(i, _):
        beyond = jnp.where(i == 0, north, 0.0)
        smooth_rows(t_ref, sides, root_ref, band_ref, s_ref, parts, count * i, count, count * i, (0, beyond))
        return 0

    lax.fori_loop(0, 2, rows, 0)
    square_ref[...] = sum(parts[pl.ds(m, TOP, stride=8), :] for m in range(8))


def smooth_bottom_kernel(t_ref, side_ref, south_ref, root_ref, band_ref, s_ref, square_ref, parts):
    count = (N - TOP) // 2

    def rows(i, _):
        beyond = jnp.where(i == 1, south_ref[...], 0.0)
        row = TOP + count * i
        smooth_rows(t_ref, side_ref[...], root_ref, band_ref, s_ref, parts, row, count, count * i, (count - 1, beyond))
        return 0

    lax.fori_loop(0, 2, rows, 0)
    square_ref[...] = sum(parts[pl.ds(m, N - TOP, stride=8), :] for m in range(8))


def final_kernel(p0, p1, p2, p3, s0_ref, s1_ref, square0, square1, lab_ref, own_ref, root_ref, out_ref, e_ref, cross_ref):
    own = own_ref[...]
    lefts, rights = [], []
    for p in (p0, p1, p2, p3):
        pay = p[...]
        gl = pay[LEV + 2 : LEV + 3].astype(F32) * 64.0 + pay[LEV + 3 : LEV + 4].astype(F32)
        lefts.append(pay)
        rights.append(jnp.where(own == gl, 1.0, 0.0).astype(BF16))
    total = dot(jnp.concatenate(lefts, axis=1), jnp.concatenate(rights, axis=1), NT)
    count = 256.0 * total[LEV : LEV + 1] + 32.0 * total[LEV + 1 : LEV + 2]
    profile = root_ref[...] * (total * (8.0 / jnp.maximum(count, 1.0)))
    hi = profile.astype(BF16).astype(F32)
    lo = (profile - hi).astype(BF16).astype(F32)
    profile = hi + lo
    energy = jnp.sum(profile * profile, axis=0, keepdims=True)
    energy_hi = energy.astype(BF16).astype(F32)
    row = iota((KA, N), 0)
    hi = jnp.where(row == LEV, energy_hi, hi).astype(BF16)
    lo = jnp.where(row == LEV, energy - energy_hi, lo).astype(BF16)
    left = jnp.concatenate([hi, lo], axis=1)
    ids = iota((N, N), 0).astype(F32).astype(BF16)

    def patch_row(q, s_ref, top):
        row = lab_ref[pl.ds(4 * q, 1), :].astype(F32).astype(BF16)
        mark = jnp.where(row == ids, BF16(1.0), BF16(0.0))
        placed = dot(left, jnp.concatenate([mark, mark], axis=0), NN)
        e_ref[pl.ds(4 * q, 4), :] = placed[LEV : LEV + 1] + jnp.zeros((4, N), F32)
        for m in range(4):
            r = 4 * q + m
            cross = s_ref[pl.ds((r - top) * KA, KA), :] * placed
            cross_ref[pl.ds(8 * r, 8), :] = jnp.sum(cross.reshape(KA // 8, 8, N), axis=0)

    for q in range(N // 4):
        if 4 * q < TOP:
            patch_row(q, s0_ref, 0)
        else:
            patch_row(q, s1_ref, TOP)
    e = e_ref[...]
    square = jnp.concatenate([square0[...], square1[...]], axis=0)
    cross = sum(cross_ref[pl.ds(m, N, stride=8), :] for m in range(8))
    out_ref[...] = jnp.sqrt(jnp.maximum(square - 2.0 * cross + e, 0.0) / e)


def vertical(turn):
    pairs = []
    for i in range(8):
        for j in range(16):
            if (j % 4 < 2) == (turn == 0):
                other = 16 * i + (j ^ 1) if i in (0, 7) else 16 * (i + 1 if i % 2 else i - 1) + j
            else:
                other = 16 * (i ^ 1) + j
            pairs.append((16 * i + j, other))
    return pairs


def params(mib):
    return pltpu.CompilerParams(vmem_limit_bytes=mib * 1024 * 1024)


def cost(flops, moved):
    return pl.CostEstimate(flops=flops, bytes_accessed=moved, transcendentals=0)


def shards(humidity, wind_u, wind_v, weights, labels, global_labels):
    vmem = pl.BlockSpec(memory_space=pltpu.VMEM)
    anywhere = pl.BlockSpec(memory_space=pl.ANY)
    edge = pltpu.VMEM((KA, N), BF16)
    wide = pltpu.VMEM((KA, N), F32)
    gl = global_labels.reshape(1, N)
    w = weights.reshape(1, LEV)
    t, s0, s1, c0, c1, band = pl.pallas_call(
        transport_kernel,
        out_shape=(pltpu.VMEM(((N + 2) * KP, N), F32), edge, edge, edge, edge, pltpu.VMEM((3 * N, 2 * N), BF16)),
        in_specs=[anywhere] * 3,
        out_specs=[vmem] * 6,
        scratch_shapes=[pltpu.VMEM((LEV, N, N), BF16)] * 3
        + [pltpu.VMEM((3, N, N), BF16), pltpu.VMEM((N, N), BF16), pltpu.VMEM((2, KA, 3 * N), BF16)]
        + [pltpu.SemaphoreType.DMA((len(CHUNKS), 3))],
        compiler_params=params(18),
        cost_estimate=cost(30_000_000, 23_000_000),
        name="transport",
    )(*(pltpu.with_memory_space_constraint(x, pltpu.HBM) for x in (humidity, wind_u, wind_v)))
    r0 = lax.ppermute(s0, ("lat", "lon"), vertical(0))
    r1 = lax.ppermute(s1, ("lat", "lon"), vertical(1))
    ro = lax.ppermute(c1, "lon", [(j, (j + 1) % 16 if j % 2 else (j - 1) % 16) for j in range(16)])
    rc = lax.ppermute(c0, "lon", [(j, j ^ 1) for j in range(16)])
    t0, root, own, marks = pl.pallas_call(
        sums_kernel,
        out_shape=(wide, wide, pltpu.VMEM((N, N), F32), pltpu.VMEM((N, 4 * N), BF16)),
        in_specs=[vmem] * 4,
        out_specs=[vmem] * 4,
        scratch_shapes=[pltpu.VMEM((N, N), jnp.int32)] * 2,
        compiler_params=params(8),
        cost_estimate=cost(600_000_000, 9_500_000),
        name="sums",
    )(t, labels, gl, w)
    pay = pl.pallas_call(
        pack_kernel,
        out_shape=edge,
        in_specs=[vmem] * 6,
        out_specs=vmem,
        compiler_params=params(8),
        cost_estimate=cost(20_000_000, 300_000),
        name="pack",
    )(t0, r0, r1, ro, rc, marks)
    p2 = lax.ppermute(pay, "lat", [(i, (i + 4) % 8) for i in range(8)])
    p1 = lax.ppermute(pay, "lon", [(j, j ^ 1) for j in range(16)])
    p3 = lax.ppermute(p2, "lon", [(j, j ^ 1) for j in range(16)])
    top0, square0, side, south = pl.pallas_call(
        smooth_top_kernel,
        out_shape=(pltpu.VMEM((TOP * KA, N), F32), pltpu.VMEM((TOP, N), F32), edge, wide),
        in_specs=[vmem] * 7,
        out_specs=[vmem] * 4,
        scratch_shapes=[pltpu.VMEM((2 * KA, N), BF16), pltpu.VMEM((8 * TOP, N), F32)],
        compiler_params=params(12),
        cost_estimate=cost(600_000_000, 9_500_000),
        name="smooth_top",
    )(t, r0, r1, rc, ro, root, band)
    bottom, square1 = pl.pallas_call(
        smooth_bottom_kernel,
        out_shape=(pltpu.VMEM(((N - TOP) * KA, N), F32), pltpu.VMEM((N - TOP, N), F32)),
        in_specs=[vmem] * 5,
        out_specs=[vmem] * 2,
        scratch_shapes=[pltpu.VMEM((8 * (N - TOP), N), F32)],
        compiler_params=params(12),
        cost_estimate=cost(600_000_000, 9_500_000),
        name="smooth_bottom",
    )(t, side, south, root, band)
    return pl.pallas_call(
        final_kernel,
        out_shape=jax.ShapeDtypeStruct((N, N), F32),
        in_specs=[vmem] * 11,
        out_specs=vmem,
        scratch_shapes=[pltpu.VMEM((N, N), F32), pltpu.VMEM((8 * N, N), F32)],
        compiler_params=params(8),
        cost_estimate=cost(300_000_000, 9_500_000),
        name="final",
    )(pay, p1, p2, p3, top0, bottom, square0, square1, labels, own, root)


def solution(mesh):
    return jax.shard_map(
        shards,
        mesh=mesh,
        in_specs=(
            P(None, "lat", "lon"),
            P(None, "lat", "lon"),
            P(None, "lat", "lon"),
            P(),
            P("lat", "lon"),
            P("lat", "lon", None),
        ),
        out_specs=P("lat", "lon"),
        check_vma=False,
    )
```
